32 devices in a mesh: grp: 2 (over y), blk: 4 (over z), ch: 2 (over x), sub: 2 (over core).
Axes of the slice: x: 2, y: 2, z: 4, core: 2. Of those that a mesh axis runs over, the one named last changes fastest.
Arguments:
- pair_in: bfloat16 [192, 96, 128], P(('grp', 'blk', 'sub'), 'ch'), parts along dimension 0, may hold values from -6 to 6
- cotangent: bfloat16 [192, 96, 128], P(('grp', 'blk', 'sub'), 'ch'), parts along dimension 0, may hold values from -6 to 6
- chain_ids: int32 [192], P('grp'), parts along dimension 0, may hold values from 0 to 3, never falling along the last dimension, each value on 1 to 48 neighbouring positions
- live_length: int32 [2], P('grp'), parts along dimension 0, may hold values from 48 to 96
- chain_embed: float32 [128], replicated, may hold values from -4 to 4
- gain_in: float32 [128], replicated, may hold values from 0.5 to 1.5
- bias_in: float32 [128], replicated, may hold values from -3 to 3
- w_proj: bfloat16 [128, 256], replicated, may hold values from -0.5 to 0.5
- w_gate: bfloat16 [128, 256], replicated, may hold values from -0.5 to 0.5
- w_gout: bfloat16 [128, 128], replicated, may hold values from -0.5 to 0.5
- gain_out: float32 [128], replicated, may hold values from 0.5 to 1.5
- bias_out: float32 [128], replicated, may hold values from -3 to 3
- w_out: bfloat16 [128, 128], replicated, may hold values from -0.5 to 0.5
Outputs:
- new_pair: bfloat16 [192, 96, 128], P(('grp', 'blk', 'sub'), 'ch'), parts along dimension 0
- pair_cols: bfloat16 [192, 96, 128], P(('grp', 'blk', 'sub'), None, 'ch'), parts along dimension 0
- grad_pair: float32 [192, 96, 128], P(('grp', 'blk', 'sub'), 'ch'), parts along dimension 0
- grad_w_proj: float32 [256, 256], P('grp'), parts along dimension 0
- grad_w_gate: float32 [256, 256], P('grp'), parts along dimension 0
- grad_w_gout: float32 [256, 128], P('grp'), parts along dimension 0
- grad_w_out: float32 [256, 128], P('grp'), parts along dimension 0
The draws below stay inside these ranges and needn't reach their ends.
There are 2 independent parts, one for each index of `grp`. The reference program is written for one: setup_inputs(seed, part) draws one part's arguments, and reference() takes and returns one part's arrays. A program takes and returns all parts, laid end to end along the dimension named above; an argument that names none is the same for every part. Nothing has to cross between parts.
All inputs are finite; a program needn't handle non-finite values.
Results may differ from the reference program's by a relative error of at most 0.0061.
Values may be sent and summed in bfloat16 or wider, within the bound.
A program may use at most 64 MiB of HBM per device.

```python
import math
import jax
import jax.numpy as jnp
import numpy as np
from jax import lax

C = 128
TOKENS = 96


def shard_levels(own_key, shape, split, low, top_value):
    def one(position, blocks):
        heights = jax.random.uniform(jax.random.fold_in(jax.random.fold_in(own_key, 6), position), (blocks,), jnp.float32, low / len(split), top_value / len(split))
        return jnp.repeat(jnp.exp(heights), shape[position] // blocks).reshape((-1,) + (1,) * (len(shape) - position - 1))

    level = one(*split[0])
    for cut in split[1:]:
        level = level * one(*cut)
    return level


def length_profile(amount, total, bound, lean):
    loads = [(1 << 20) // math.isqrt(grade ** lean) + 1 for grade in range(2, amount + 1)]
    surplus, given = total - bound - (amount - 1), [1] * (amount - 1)
    while surplus > 0:
        candidates = [i for i in range(amount - 1) if given[i] < bound]
        whole, left = sum([loads[i] for i in candidates]), surplus
        for i in candidates:
            more = min(bound - given[i], max(1, left * loads[i] // whole), surplus)
            given[i] = given[i] + more
            surplus = surplus - more
    return np.array([bound] + given)


def uneven_parts(key, count, total, limit, lean):
    if count == 2:
        one = jax.random.randint(key, (), max(1, total - limit), min(limit, total - 1) + 1)
        return jnp.stack([one, total - one])
    lengths = jnp.asarray(length_profile(count, total, limit, lean), jnp.int32)
    couples = (count - 1) // 2
    donor, receiver = lengths[1:1 + 2 * couples:2], lengths[2:2 + 2 * couples:2]
    room = jnp.minimum(donor - 1, limit - receiver)
    shifted = jax.random.randint(jax.random.fold_in(key, 1), (couples,), 0, 1 << 20) % (room + 1)
    lengths = lengths.at[1:1 + 2 * couples:2].set(donor - shifted).at[2:2 + 2 * couples:2].set(receiver + shifted)
    return lengths[jax.random.permutation(jax.random.fold_in(key, 2), count)]


def scatter_about(rng, dims, scale, reach, pieces=(), kind=jnp.bfloat16):
    drawn = scale * jax.random.normal(rng, dims, jnp.float32)
    if pieces:
        drawn = drawn * shard_levels(rng, dims, pieces, -0.22, 0.18)
    return jnp.clip(drawn, -reach, reach).astype(kind)


def setup_inputs(seed: int = 0, part: int = 0) -> dict:
    key_of = jax.random.split(jax.random.key(seed), 14)
    part_splits = jax.random.split(jax.random.fold_in(key_of[13], part), 14)
    pair_in = scatter_about(part_splits[0], (TOKENS, TOKENS, C), 1.0, 6.0, ((0, 8), (1, 2)))
    cotangent = scatter_about(part_splits[1], (TOKENS, TOKENS, C), 1.0, 6.0, ((0, 8), (1, 2)))
    chain_ids = jnp.searchsorted(jnp.cumsum(uneven_parts(part_splits[2], 4, TOKENS, TOKENS // 2, 0)), jnp.arange(TOKENS), side="right").astype(jnp.int32)
    live_length = jax.random.randint(part_splits[3], (1,), TOKENS // 2, TOKENS + 1).astype(jnp.int32)
    chain_embed = scatter_about(key_of[4], (C,), 1.0, 4.0, (), jnp.float32)
    gain_in = jnp.clip(1.0 + 0.1 * jax.random.normal(key_of[5], (C,), jnp.float32), 0.5, 1.5)
    bias_in = scatter_about(key_of[6], (C,), 0.5, 3.0, (), jnp.float32)
    w_proj = scatter_about(key_of[7], (C, 2 * C), C ** -0.5, 0.5)
    w_gate = scatter_about(key_of[8], (C, 2 * C), C ** -0.5, 0.5)
    w_gout = scatter_about(key_of[9], (C, C), C ** -0.5, 0.5)
    gain_out = jnp.clip(1.0 + 0.1 * jax.random.normal(key_of[10], (C,), jnp.float32), 0.5, 1.5)
    bias_out = scatter_about(key_of[11], (C,), 0.5, 3.0, (), jnp.float32)
    w_out = scatter_about(key_of[12], (C, C), C ** -0.5, 0.5)
    return dict(pair_in=pair_in, cotangent=cotangent, chain_ids=chain_ids, live_length=live_length, chain_embed=chain_embed, gain_in=gain_in, bias_in=bias_in, w_proj=w_proj, w_gate=w_gate, w_gout=w_gout, gain_out=gain_out, bias_out=bias_out, w_out=w_out)


eps = 1e-05

def norm_affine(field, gain, bias):
    mean = lax.optimization_barrier(jnp.mean(field, axis=-1, keepdims=True))
    centred = field - mean
    spread = lax.optimization_barrier(jnp.mean(centred * centred, axis=-1, keepdims=True))
    return centred * lax.rsqrt(spread + eps) * gain + bias

def flat_grad(left_cells, right_cells, width_left, width_right):
    return jnp.dot(left_cells.reshape(-1, width_left).astype(jnp.float32).T, right_cells.reshape(-1, width_right), precision=lax.Precision.HIGHEST)

def reference(pair_in, cotangent, chain_ids, live_length, chain_embed, gain_in, bias_in, w_proj, w_gate, w_gout, gain_out, bias_out, w_out):
    count = pair_in.shape[0]
    width = pair_in.shape[2]
    positions = jnp.arange(count, dtype=jnp.int32)
    live = (positions < live_length[0]).astype(jnp.float32)
    cell_mask = (live[:, None] * live[None, :])[..., None]
    same = (chain_ids[:, None] == chain_ids[None, :]).astype(jnp.float32)
    pair = pair_in.astype(jnp.float32) + same[..., None] * chain_embed
    normed, back_in = jax.vjp(lambda field: norm_affine(field, gain_in, bias_in), pair)
    normed_cast = normed.astype(jnp.bfloat16)
    projected = jnp.dot(normed_cast, w_proj, preferred_element_type=jnp.float32)
    gate_pre = jnp.dot(normed_cast, w_gate, preferred_element_type=jnp.float32)
    gout_pre = jnp.dot(normed_cast, w_gout, preferred_element_type=jnp.float32)
    gate_sig = jax.nn.sigmoid(gate_pre)
    gout = jax.nn.sigmoid(gout_pre)
    operands = (projected * gate_sig * cell_mask).astype(jnp.bfloat16)
    left = operands[..., :width].astype(jnp.float32)
    right = operands[..., width:].astype(jnp.float32)
    tri = jnp.einsum('ikc,jkc->ijc', left, right, precision=lax.Precision.HIGHEST).astype(jnp.bfloat16)
    outnorm, back_out = jax.vjp(lambda field: norm_affine(field, gain_out, bias_out), tri.astype(jnp.float32))
    outnorm_cast = outnorm.astype(jnp.bfloat16)
    out_lin = jnp.dot(outnorm_cast, w_out, preferred_element_type=jnp.float32)
    new_pair = (pair + out_lin * gout).astype(jnp.bfloat16)
    pair_cols = jnp.transpose(new_pair, (1, 0, 2))
    d_new = cotangent.astype(jnp.float32)
    d_lin = d_new * gout
    d_gout_pre = d_new * out_lin * gout * (1.0 - gout)
    grad_w_out = flat_grad(outnorm_cast, d_lin, width, width)
    d_norm = jnp.dot(d_lin, w_out.astype(jnp.float32).T, precision=lax.Precision.HIGHEST)
    d_tri, = back_out(d_norm)
    d_tri = d_tri.astype(jnp.bfloat16).astype(jnp.float32)
    d_left = jnp.einsum('ijc,jkc->ikc', d_tri, right, precision=lax.Precision.HIGHEST).astype(jnp.bfloat16)
    d_right = jnp.einsum('ijc,ikc->jkc', d_tri, left, precision=lax.Precision.HIGHEST).astype(jnp.bfloat16)
    d_operands = jnp.concatenate([d_left, d_right], axis=-1).astype(jnp.float32)
    d_proj = d_operands * gate_sig * cell_mask
    d_gate = d_operands * projected * gate_sig * (1.0 - gate_sig) * cell_mask
    grad_w_proj = flat_grad(normed_cast, d_proj, width, 2 * width)
    grad_w_gate = flat_grad(normed_cast, d_gate, width, 2 * width)
    grad_w_gout = flat_grad(normed_cast, d_gout_pre, width, width)
    highest = lax.Precision.HIGHEST
    d_normed = jnp.dot(d_proj, w_proj.astype(jnp.float32).T, precision=highest)
    d_normed = d_normed + jnp.dot(d_gate, w_gate.astype(jnp.float32).T, precision=highest)
    d_normed = d_normed + jnp.dot(d_gout_pre, w_gout.astype(jnp.float32).T, precision=highest)
    d_pair, = back_in(d_normed)
    grad_pair = d_new + d_pair
    return (new_pair, pair_cols, grad_pair, grad_w_proj, grad_w_gate, grad_w_gout, grad_w_out)
```

```python
import functools

import jax
import jax.numpy as jnp
from jax import lax
from jax.experimental import pallas as pl
from jax.experimental.pallas import tpu as pltpu
from jax.sharding import PartitionSpec as P

eps = 1e-05


def norm_affine(field, gain, bias):
    mean = jnp.mean(field, axis=-1, keepdims=True)
    centred = field - mean
    spread = jnp.mean(centred * centred, axis=-1, keepdims=True)
    return centred * lax.rsqrt(spread + eps) * gain + bias


def flat_grad(left_cells, right_cells, width_left, width_right):
    left_flat = left_cells.reshape(-1, width_left)
    right_flat = right_cells.reshape(-1, width_right)
    right_high = right_flat.astype(jnp.bfloat16)
    right_low = (right_flat - right_high.astype(jnp.float32)).astype(jnp.bfloat16)
    dims = (((0,), (0,)), ((), ()))
    upper = lax.dot_general(left_flat, right_high, dims, preferred_element_type=jnp.float32)
    lower = lax.dot_general(left_flat, right_low, dims, preferred_element_type=jnp.float32)
    return upper + lower


def fold_right(right_ch, update, initial):
    return update(
        initial, lax.all_gather(right_ch, ("blk", "sub"), axis=0, tiled=True), jnp.int32(0)
    )


def on_device(
    pair_in,
    cotangent,
    chain_ids,
    live_length,
    chain_embed,
    gain_in,
    bias_in,
    w_proj,
    w_gate,
    w_gout,
    gain_out,
    bias_out,
    w_out,
):
    row_count = pair_in.shape[0]
    col_count = pair_in.shape[1]
    width = pair_in.shape[2]
    row_start = lax.axis_index(("blk", "sub")) * row_count
    col_start = lax.axis_index("ch") * col_count
    row_pos = row_start + jnp.arange(row_count, dtype=jnp.int32)
    col_pos = col_start + jnp.arange(col_count, dtype=jnp.int32)
    live_rows = (row_pos < live_length[0]).astype(jnp.float32)
    live_cols = (col_pos < live_length[0]).astype(jnp.float32)
    cell_mask = (live_rows[:, None] * live_cols[None, :])[..., None]
    chain_rows = lax.dynamic_slice_in_dim(chain_ids, row_start, row_count)
    chain_cols = lax.dynamic_slice_in_dim(chain_ids, col_start, col_count)
    same = (chain_rows[:, None] == chain_cols[None, :]).astype(jnp.float32)
    pair = pair_in.astype(jnp.float32) + same[..., None] * chain_embed
    normed, back_in = jax.vjp(lambda field: norm_affine(field, gain_in, bias_in), pair)
    normed_cast = normed.astype(jnp.bfloat16)
    projected = jnp.dot(normed_cast, w_proj, preferred_element_type=jnp.float32)
    gate_pre = jnp.dot(normed_cast, w_gate, preferred_element_type=jnp.float32)
    gout_pre = jnp.dot(normed_cast, w_gout, preferred_element_type=jnp.float32)
    gate_sig = jax.nn.sigmoid(gate_pre)
    gout = jax.nn.sigmoid(gout_pre)
    operands = (projected * gate_sig * cell_mask).astype(jnp.bfloat16)
    left_ch, right_ch = (
        lax.all_to_all(operands[..., :width], "ch", split_axis=2, concat_axis=1, tiled=True),
        lax.all_to_all(operands[..., width:], "ch", split_axis=2, concat_axis=1, tiled=True),
    )

    def add_tri(carry, piece, start):
        update = jnp.einsum("ikc,jkc->ijc", left_ch, piece, preferred_element_type=jnp.float32)
        return update

    tri_sum = fold_right(right_ch, add_tri, jnp.zeros(left_ch.shape, jnp.float32))
    tri_cast = tri_sum.astype(jnp.bfloat16)
    tri_cells = lax.all_to_all(tri_cast, "ch", split_axis=1, concat_axis=2, tiled=True)
    outnorm, back_out = jax.vjp(
        lambda field: norm_affine(field, gain_out, bias_out), tri_cells.astype(jnp.float32)
    )
    outnorm_cast = outnorm.astype(jnp.bfloat16)
    out_lin = jnp.dot(outnorm_cast, w_out, preferred_element_type=jnp.float32)
    new_pair = (pair + out_lin * gout).astype(jnp.bfloat16)
    swapped = lax.all_to_all(
        lax.all_to_all(new_pair, "ch", split_axis=2, concat_axis=1, tiled=True),
        ("blk", "sub"),
        split_axis=1,
        concat_axis=0,
        tiled=True,
    )
    pair_cols = jnp.transpose(swapped, (1, 0, 2))
    d_new = cotangent.astype(jnp.float32)
    d_lin = d_new * gout
    d_gout_pre = d_new * out_lin * gout * (1.0 - gout)
    local_w_out = flat_grad(outnorm_cast, d_lin, width, width)
    d_norm = jnp.dot(d_lin, w_out.astype(jnp.float32).T, precision=lax.Precision.HIGHEST)
    (d_tri,) = back_out(d_norm)
    d_tri_cast = d_tri.astype(jnp.bfloat16)
    d_tri_ch = lax.all_to_all(d_tri_cast, "ch", split_axis=2, concat_axis=1, tiled=True)

    def add_left(carry, piece, start):
        return jnp.einsum("ijc,jkc->ikc", d_tri_ch, piece, preferred_element_type=jnp.float32)

    d_left = fold_right(right_ch, add_left, jnp.zeros(left_ch.shape, jnp.float32))
    d_tri_swap = lax.all_to_all(d_tri_ch, ("blk", "sub"), split_axis=1, concat_axis=0, tiled=True)
    d_right = jnp.einsum(
        "ijc,ikc->jkc",
        d_tri_swap,
        lax.all_gather(left_ch, ("blk", "sub"), axis=0, tiled=True),
        preferred_element_type=jnp.float32,
    )
    back_left, back_right = (
        lax.all_to_all(d_left.astype(jnp.bfloat16), "ch", split_axis=1, concat_axis=2, tiled=True),
        lax.all_to_all(d_right.astype(jnp.bfloat16), "ch", split_axis=1, concat_axis=2, tiled=True),
    )
    d_operands = jnp.concatenate([back_left, back_right], axis=-1).astype(jnp.float32)
    d_proj = d_operands * gate_sig * cell_mask
    d_gate = d_operands * projected * gate_sig * (1.0 - gate_sig) * cell_mask
    local_w_proj = flat_grad(normed_cast, d_proj, width, 2 * width)
    local_w_gate = flat_grad(normed_cast, d_gate, width, 2 * width)
    local_w_gout = flat_grad(normed_cast, d_gout_pre, width, width)
    highest = lax.Precision.HIGHEST
    d_normed = jnp.dot(d_proj, w_proj.astype(jnp.float32).T, precision=highest)
    d_normed = d_normed + jnp.dot(d_gate, w_gate.astype(jnp.float32).T, precision=highest)
    d_normed = d_normed + jnp.dot(d_gout_pre, w_gout.astype(jnp.float32).T, precision=highest)
    (d_pair,) = back_in(d_normed)
    grad_pair = d_new + d_pair
    grad_w_proj, grad_w_gate, grad_w_gout, grad_w_out = lax.psum(
        (local_w_proj, local_w_gate, local_w_gout, local_w_out), ("blk", "ch", "sub")
    )
    return (new_pair, pair_cols, grad_pair, grad_w_proj, grad_w_gate, grad_w_gout, grad_w_out)


OPS, TRI, DTRI, DOPS, RS_A, AG_A, RS_B, AG_B, PHASES = range(9)


def column_norm(field):
    mean = jnp.mean(field, axis=0, keepdims=True)
    centred = field - mean
    spread = jnp.mean(centred * centred, axis=0, keepdims=True)
    scale = lax.rsqrt(spread + eps)
    return centred * scale, scale


def column_norm_back(unit, scale, d_unit):
    first = jnp.mean(d_unit, axis=0, keepdims=True)
    second = jnp.mean(d_unit * unit, axis=0, keepdims=True)
    return scale * (d_unit - first - unit * second)


def matmul(a, b, dims=((1,), (0,))):
    return lax.dot_general(a, b, (dims, ((), ())), preferred_element_type=jnp.float32)


def low(x):
    return x.astype(jnp.bfloat16)


def wide(x):
    return x.astype(jnp.float32)


def kernel(
    sizes,
    rows,
    cols,
    live_ref,
    pair_ref,
    cot_ref,
    chain_ref,
    embed_ref,
    gain_in_ref,
    bias_in_ref,
    gain_out_ref,
    bias_out_ref,
    w_proj_ref,
    w_gate_ref,
    w_gout_ref,
    w_out_ref,
    new_ref,
    swapped_ref,
    grad_ref,
    g_proj_ref,
    g_gate_ref,
    g_gout_ref,
    g_out_ref,
    s_ops, r_ops, s_tri, r_tri, s_dtri, r_dtri, s_dops, r_dops,
    s_rsa, r_rsa, s_aga, r_aga, s_rsb, r_rsb, s_agb, r_agb,
    s_col, r_col,
    pair_buf, normed_buf, proj_buf, gate_buf, gout_buf, dlin_buf, dnew_buf, dgout_buf,
    pairs16, pairs8, left_buf, right_buf, flat16, flat8, cells_buf, rows_buf, col_f32, swap_f32,
    send_sem, recv_sem, col_send, col_recv,
):
    nblk, nsub, nch = sizes["blk"], sizes["sub"], sizes["ch"]
    n = nblk * nsub * nch
    width = pair_ref.shape[1]
    per = width // n
    cells = rows * cols
    half = cells // 2
    half_rows = rows // 2
    tokens = cols * nch
    my_row = lax.axis_index("blk") * nsub + lax.axis_index("sub")
    my_ch = lax.axis_index("ch")
    me = my_row * nch + my_ch

    def place(row, col):
        return {"blk": row // nsub, "sub": row % nsub, "ch": col}

    def start(phase, src_of, dst):
        copies = []
        for t in range(1, n):
            q = (me + t) % n
            copy = pltpu.make_async_remote_copy(
                src_ref=src_of(q),
                dst_ref=dst.at[me],
                send_sem=send_sem.at[phase, t],
                recv_sem=recv_sem.at[phase, t],
                device_id=place(q // nch, q % nch),
                device_id_type=pl.DeviceIdType.MESH,
            )
            copy.start()
            copies.append(copy)
        return copies

    def arrive(phase, copies, dst):
        for t in range(1, n):
            q = (me + n - t) % n
            pltpu.make_async_remote_copy(
                src_ref=dst.at[q],
                dst_ref=dst.at[q],
                send_sem=send_sem.at[phase, t],
                recv_sem=recv_sem.at[phase, t],
                device_id=place(q // nch, q % nch),
                device_id_type=pl.DeviceIdType.MESH,
            ).wait_recv()

    sent = []

    def exchange(phase, src, dst):
        sent.extend(start(phase, lambda q: src.at[q], dst))
        dst[me] = src[me]

    barrier = pltpu.get_barrier_semaphore()
    for t in range(1, n):
        q = (me + t) % n
        pl.semaphore_signal(
            barrier,
            inc=1,
            device_id=place(q // nch, q % nch),
            device_id_type=pl.DeviceIdType.MESH,
        )

    vectors = jnp.concatenate(
        [
            embed_ref[...],
            gain_in_ref[...],
            bias_in_ref[...],
            gain_out_ref[...],
            bias_out_ref[...],
            jnp.zeros((3, width), jnp.float32),
        ],
        axis=0,
    ).T
    embed, gain_in, bias_in, gain_out, bias_out = [vectors[:, q : q + 1] for q in range(5)]

    cell = lax.broadcasted_iota(jnp.int32, (tokens, cells), 1)
    token = lax.broadcasted_iota(jnp.int32, (tokens, cells), 0)
    local_row = jnp.zeros((tokens, cells), jnp.int32)
    for q in range(1, rows):
        local_row = local_row + (cell >= q * cols).astype(jnp.int32)
    row_pos = my_row * rows + local_row
    col_pos = my_ch * cols + cell - local_row * cols
    pick = (token == row_pos).astype(jnp.float32) - (token == col_pos).astype(jnp.float32)
    chain = jnp.broadcast_to(wide(chain_ref[...]), (8, tokens))
    apart = matmul(low(chain), low(pick))[0:1]
    same = (apart == 0.0).astype(jnp.float32)
    length = live_ref[0, 0]
    mask = (row_pos[0:1] < length).astype(jnp.float32) * (col_pos[0:1] < length).astype(jnp.float32)

    pair = wide(pair_ref[...]).T + same * embed
    pair_buf[...] = pair
    unit_in, scale_in = column_norm(pair)
    normed = low(unit_in * gain_in + bias_in)
    normed_buf[...] = normed
    projected = matmul(low(wide(w_proj_ref[...]).T), normed)
    gate_sig = jax.nn.sigmoid(matmul(low(wide(w_gate_ref[...]).T), normed))
    masked = gate_sig * mask
    operands = projected * masked
    gate_buf[...] = masked
    proj_buf[...] = operands * (1.0 - gate_sig)
    for q in range(n):
        low_q, high_q = q * per, width + q * per
        s_ops[q] = low(
            jnp.concatenate(
                [operands[low_q : low_q + per], operands[high_q : high_q + per]], axis=0
            )
        )
    pl.semaphore_wait(barrier, n - 1)
    exchange(OPS, s_ops, r_ops)

    gout = jax.nn.sigmoid(matmul(low(wide(w_gout_ref[...]).T), normed))
    gout_buf[...] = gout
    d_new = wide(cot_ref[...]).T
    dnew_buf[...] = d_new
    d_lin = low(d_new * gout)
    dlin_buf[...] = d_lin
    d_unit_out = matmul(w_out_ref[...], d_lin) * gain_out
    w_out_t = low(wide(w_out_ref[...]).T)

    arrive(OPS, None, r_ops)
    for q in range(n):
        block_row, block_col = q // nch, q % nch
        x = wide(r_ops[q])
        for i in range(rows):
            at = (block_row * rows + i) * 2 * per
            pairs16[at : at + 2 * per, block_col * cols : (block_col + 1) * cols] = x[
                :, i * cols : (i + 1) * cols
            ]
    for c in range(per):
        left = low(pairs16[pl.ds(c, tokens, stride=2 * per), :])
        right = low(pairs16[pl.ds(per + c, tokens, stride=2 * per), :])
        left_buf[c] = left
        right_buf[c] = right
        pairs8[pl.ds(c, tokens, stride=per), :] = matmul(left, right, ((1,), (1,)))
    for q in range(n):
        block_row, block_col = q // nch, q % nch
        for i in range(rows):
            at = (block_row * rows + i) * per
            down, along = (i // half_rows) * per, (i % half_rows) * cols
            flat8[q, down : down + per, along : along + cols] = pairs8[
                at : at + per, block_col * cols : (block_col + 1) * cols
            ]
        s_tri[q] = low(flat8[q])
    exchange(TRI, s_tri, r_tri)
    arrive(TRI, None, r_tri)
    for q in range(n):
        x = wide(r_tri[q])
        cells_buf[q * per : (q + 1) * per, 0:half] = x[0:per]
        cells_buf[q * per : (q + 1) * per, half:cells] = x[per : 2 * per]

    unit_out, scale_out = column_norm(cells_buf[...])
    d_tri = column_norm_back(unit_out, scale_out, d_unit_out)
    for q in range(n):
        x = d_tri[q * per : (q + 1) * per]
        s_dtri[q] = low(jnp.concatenate([x[:, 0:half], x[:, half:cells]], axis=0))
    exchange(DTRI, s_dtri, r_dtri)

    outnorm = low(unit_out * gain_out + bias_out)
    out_lin = matmul(w_out_t, outnorm)
    gout = gout_buf[...]
    moved = out_lin * gout
    d_gout = low(dnew_buf[...] * moved * (1.0 - gout))
    dgout_buf[...] = d_gout
    grad_gout = matmul(normed_buf[...], d_gout, ((1,), (1,)))
    grad_out = matmul(outnorm, dlin_buf[...], ((1,), (1,)))
    for q in range(n):
        at = q * per
        s_rsa[q] = low(
            jnp.concatenate([grad_gout[at : at + per], grad_out[at : at + per]], axis=0)
        )
    exchange(RS_A, s_rsa, r_rsa)

    rows_buf[...] = (pair_buf[...] + moved).T
    new_ref[...] = low(rows_buf[...])
    share = cols // rows
    lanes = width // nch
    first = lax.broadcasted_iota(jnp.int32, (rows, width), 1) < lanes
    for m in range(share):
        for j in range(half_rows):
            a = rows_buf[pl.ds(m * rows + j, rows, stride=cols), :]
            b = rows_buf[pl.ds(m * rows + j + half_rows, rows, stride=cols), :]
            col_f32[m * nch, j * rows : (j + 1) * rows, :] = jnp.where(
                first, a, pltpu.roll(b, lanes, 1)
            )
            col_f32[m * nch + 1, j * rows : (j + 1) * rows, :] = jnp.where(
                first, pltpu.roll(a, lanes, 1), b
            )
        for col in range(nch):
            used = half_rows * rows
            spare = col_f32.shape[1] - used
            if spare:
                col_f32[m * nch + col, used : used + spare, :] = jnp.zeros(
                    (spare, width), jnp.float32
                )
            s_col[m * nch + col] = low(col_f32[m * nch + col])

    def col_copy(slot, row, col):
        return pltpu.make_async_remote_copy(
            src_ref=s_col.at[slot],
            dst_ref=r_col.at[my_row],
            send_sem=col_send.at[slot],
            recv_sem=col_recv.at[my_row],
            device_id=place(row, col),
            device_id_type=pl.DeviceIdType.MESH,
        )

    for m in range(share):
        for col in range(nch):
            slot = m * nch + col
            row = my_ch * share + m
            here = row * nch + col == me

            @pl.when(here)
            def _():
                r_col[my_row] = s_col[slot]

            @pl.when(jnp.logical_not(here))
            def _():
                col_copy(slot, row, col).start()

    arrive(DTRI, None, r_dtri)
    for q in range(n):
        block_row, block_col = q // nch, q % nch
        x = wide(r_dtri[q])
        for i in range(rows):
            at = (block_row * rows + i) * per
            down, along = (i // half_rows) * per, (i % half_rows) * cols
            pairs8[at : at + per, block_col * cols : (block_col + 1) * cols] = x[
                down : down + per, along : along + cols
            ]
    for c in range(per):
        grad = pairs8[pl.ds(c, tokens, stride=per), :]
        pairs16[pl.ds(c, tokens, stride=2 * per), :] = matmul(low(grad), right_buf[c])
        pairs16[pl.ds(per + c, tokens, stride=2 * per), :] = matmul(low(grad.T), left_buf[c])
    for q in range(n):
        block_row, block_col = q // nch, q % nch
        for i in range(rows):
            at = (block_row * rows + i) * 2 * per
            flat16[q, :, i * cols : (i + 1) * cols] = pairs16[
                at : at + 2 * per, block_col * cols : (block_col + 1) * cols
            ]
        s_dops[q] = low(flat16[q])
    exchange(DOPS, s_dops, r_dops)

    def summed(buf):
        total = wide(buf[0])
        for q in range(1, n):
            total = total + wide(buf[q])
        return low(total)

    arrive(RS_A, None, r_rsa)
    s_aga[...] = summed(r_rsa)
    sent.extend(start(AG_A, lambda q: s_aga, r_aga))
    r_aga[me] = s_aga[...]

    for row in range(nblk * nsub):
        source = row * nch + my_row // share

        @pl.when(source != me)
        def _():
            pltpu.make_async_remote_copy(
                src_ref=r_col.at[row],
                dst_ref=r_col.at[row],
                send_sem=col_send.at[0],
                recv_sem=col_recv.at[row],
                device_id=place(row, my_row // share),
                device_id_type=pl.DeviceIdType.MESH,
            ).wait_recv()

        for j in range(half_rows):
            x = wide(r_col[row])[j * rows : (j + 1) * rows]
            swap_f32[j, row * rows : (row + 1) * rows, :] = x[:, 0:lanes]
            swap_f32[j + half_rows, row * rows : (row + 1) * rows, :] = x[:, lanes:width]
    swapped_ref[...] = low(swap_f32[...])
    d_normed_gout = matmul(w_gout_ref[...], dgout_buf[...])

    arrive(DOPS, None, r_dops)
    d_operands = jnp.concatenate(
        [wide(r_dops[q])[0:per] for q in range(n)]
        + [wide(r_dops[q])[per : 2 * per] for q in range(n)],
        axis=0,
    )
    d_proj = low(d_operands * gate_buf[...])
    d_gate = low(d_operands * proj_buf[...])
    normed = normed_buf[...]
    grad_proj = matmul(normed, d_proj, ((1,), (1,)))
    grad_gate = matmul(normed, d_gate, ((1,), (1,)))
    for q in range(n):
        at = q * per
        s_rsb[q] = low(
            jnp.concatenate([grad_proj[at : at + per], grad_gate[at : at + per]], axis=0)
        )
    exchange(RS_B, s_rsb, r_rsb)

    d_normed = d_normed_gout + matmul(w_proj_ref[...], d_proj) + matmul(w_gate_ref[...], d_gate)
    unit_in, scale_in = column_norm(pair_buf[...])
    d_pair = column_norm_back(unit_in, scale_in, d_normed * gain_in)
    total = dnew_buf[...] + d_pair

    arrive(RS_B, None, r_rsb)
    s_agb[...] = summed(r_rsb)
    sent.extend(start(AG_B, lambda q: s_agb, r_agb))
    r_agb[me] = s_agb[...]
    grad_ref[...] = total.T
    arrive(AG_A, None, r_aga)
    for q in range(n):
        x = wide(r_aga[q])
        g_gout_ref[q * per : (q + 1) * per, :] = x[0:per]
        g_out_ref[q * per : (q + 1) * per, :] = x[per : 2 * per]
    arrive(AG_B, None, r_agb)
    for q in range(n):
        x = wide(r_agb[q])
        g_proj_ref[q * per : (q + 1) * per, :] = x[0:per]
        g_gate_ref[q * per : (q + 1) * per, :] = x[per : 2 * per]

    for copy in sent:
        copy.wait_send()
    for m in range(share):
        for col in range(nch):
            slot = m * nch + col
            row = my_ch * share + m

            @pl.when(row * nch + col != me)
            def _():
                col_copy(slot, row, col).wait_send()


def fused(
    sizes,
    pair_in,
    cotangent,
    chain_ids,
    live_length,
    chain_embed,
    gain_in,
    bias_in,
    w_proj,
    w_gate,
    w_gout,
    gain_out,
    bias_out,
    w_out,
):
    rows, cols, width = pair_in.shape
    n = sizes["blk"] * sizes["sub"] * sizes["ch"]
    per = width // n
    cells, tokens, lanes = rows * cols, cols * sizes["ch"], width // sizes["ch"]
    half = cells // 2
    slots = cols // rows * sizes["ch"]
    col_rows = -(-(rows // 2 * rows) // 16) * 16
    bf, f32 = jnp.bfloat16, jnp.float32
    vm = pltpu.VMEM

    def both(*shape):
        return [vm((n,) + shape, bf), vm((n,) + shape, bf)]

    line = lambda x: x.reshape(1, -1)
    outs = pl.pallas_call(
        functools.partial(kernel, sizes, rows, cols),
        out_shape=(
            jax.ShapeDtypeStruct((cells, width), bf),
            jax.ShapeDtypeStruct((rows, tokens, lanes), bf),
            jax.ShapeDtypeStruct((cells, width), f32),
            jax.ShapeDtypeStruct((width, 2 * width), f32),
            jax.ShapeDtypeStruct((width, 2 * width), f32),
            jax.ShapeDtypeStruct((width, width), f32),
            jax.ShapeDtypeStruct((width, width), f32),
        ),
        in_specs=[pl.BlockSpec(memory_space=pltpu.SMEM)]
        + [pl.BlockSpec(memory_space=pltpu.VMEM)] * 12,
        out_specs=[pl.BlockSpec(memory_space=pltpu.VMEM)] * 7,
        scratch_shapes=both(2 * per, cells)
        + both(2 * per, half)
        + both(2 * per, half)
        + both(2 * per, cells)
        + both(2 * per, width)
        + [vm((2 * per, width), bf), vm((n, 2 * per, width), bf)]
        + both(2 * per, 2 * width)
        + [vm((2 * per, 2 * width), bf), vm((n, 2 * per, 2 * width), bf)]
        + [vm((slots, col_rows, width), bf), vm((n // sizes["ch"], col_rows, width), bf)]
        + [
            vm((width, cells), f32),
            vm((width, cells), bf),
            vm((2 * width, cells), f32),
            vm((2 * width, cells), f32),
            vm((width, cells), f32),
            vm((width, cells), bf),
            vm((width, cells), f32),
            vm((width, cells), bf),
            vm((tokens * 2 * per, tokens), f32),
            vm((tokens * per, tokens), f32),
            vm((per, tokens, tokens), bf),
            vm((per, tokens, tokens), bf),
            vm((n, 2 * per, cells), f32),
            vm((n, 2 * per, half), f32),
            vm((width, cells), f32),
            vm((cells, width), f32),
            vm((slots, col_rows, width), f32),
            vm((rows, tokens, lanes), f32),
            pltpu.SemaphoreType.DMA((PHASES, n)),
            pltpu.SemaphoreType.DMA((PHASES, n)),
            pltpu.SemaphoreType.DMA((slots,)),
            pltpu.SemaphoreType.DMA((n // sizes["ch"],)),
        ],
        compiler_params=pltpu.CompilerParams(
            collective_id=0, has_side_effects=True, vmem_limit_bytes=40 << 20
        ),
    )(
        line(live_length),
        pair_in.reshape(cells, width),
        cotangent.reshape(cells, width),
        line(chain_ids),
        line(chain_embed),
        line(gain_in),
        line(bias_in),
        line(gain_out),
        line(bias_out),
        w_proj,
        w_gate,
        w_gout,
        w_out,
    )
    new_pair, pair_cols, grad_pair, *grads = outs
    return (
        new_pair.reshape(rows, cols, width),
        pair_cols,
        grad_pair.reshape(rows, cols, width),
        *grads,
    )


def solution(mesh):
    sizes = dict(mesh.shape)
    devices = sizes["blk"] * sizes["sub"] * sizes["ch"]
    fits = devices * 8 == 128 and sizes["ch"] == 2
    body = functools.partial(fused, sizes) if fits else on_device
    return jax.shard_map(
        body,
        mesh=mesh,
        in_specs=(
            P(("grp", "blk", "sub"), "ch", None),
            P(("grp", "blk", "sub"), "ch", None),
            P("grp"),
            P("grp"),
            P(),
            P(),
            P(),
            P(),
            P(),
            P(),
            P(),
            P(),
            P(),
        ),
        out_specs=(
            P(("grp", "blk", "sub"), "ch", None),
            P(("grp", "blk", "sub"), None, "ch"),
            P(("grp", "blk", "sub"), "ch", None),
            P("grp", None),
            P("grp", None),
            P("grp", None),
            P("grp", None),
        ),
        check_vma=False,
    )
```

```python
import functools

import jax
import jax.numpy as jnp
from jax import lax
from jax.experimental import pallas as pl
from jax.experimental.pallas import tpu as pltpu
from jax.sharding import PartitionSpec as P

eps = 1e-05


def norm_affine(field, gain, bias):
    mean = jnp.mean(field, axis=-1, keepdims=True)
    centred = field - mean
    spread = jnp.mean(centred * centred, axis=-1, keepdims=True)
    return centred * lax.rsqrt(spread + eps) * gain + bias


def flat_grad(left_cells, right_cells, width_left, width_right):
    left_flat = left_cells.reshape(-1, width_left)
    right_flat = right_cells.reshape(-1, width_right)
    right_high = right_flat.astype(jnp.bfloat16)
    right_low = (right_flat - right_high.astype(jnp.float32)).astype(jnp.bfloat16)
    dims = (((0,), (0,)), ((), ()))
    upper = lax.dot_general(left_flat, right_high, dims, preferred_element_type=jnp.float32)
    lower = lax.dot_general(left_flat, right_low, dims, preferred_element_type=jnp.float32)
    return upper + lower


def fold_right(right_ch, update, initial):
    return update(
        initial, lax.all_gather(right_ch, ("blk", "sub"), axis=0, tiled=True), jnp.int32(0)
    )


def on_device(
    pair_in,
    cotangent,
    chain_ids,
    live_length,
    chain_embed,
    gain_in,
    bias_in,
    w_proj,
    w_gate,
    w_gout,
    gain_out,
    bias_out,
    w_out,
):
    row_count = pair_in.shape[0]
    col_count = pair_in.shape[1]
    width = pair_in.shape[2]
    row_start = lax.axis_index(("blk", "sub")) * row_count
    col_start = lax.axis_index("ch") * col_count
    row_pos = row_start + jnp.arange(row_count, dtype=jnp.int32)
    col_pos = col_start + jnp.arange(col_count, dtype=jnp.int32)
    live_rows = (row_pos < live_length[0]).astype(jnp.float32)
    live_cols = (col_pos < live_length[0]).astype(jnp.float32)
    cell_mask = (live_rows[:, None] * live_cols[None, :])[..., None]
    chain_rows = lax.dynamic_slice_in_dim(chain_ids, row_start, row_count)
    chain_cols = lax.dynamic_slice_in_dim(chain_ids, col_start, col_count)
    same = (chain_rows[:, None] == chain_cols[None, :]).astype(jnp.float32)
    pair = pair_in.astype(jnp.float32) + same[..., None] * chain_embed
    normed, back_in = jax.vjp(lambda field: norm_affine(field, gain_in, bias_in), pair)
    normed_cast = normed.astype(jnp.bfloat16)
    projected = jnp.dot(normed_cast, w_proj, preferred_element_type=jnp.float32)
    gate_pre = jnp.dot(normed_cast, w_gate, preferred_element_type=jnp.float32)
    gout_pre = jnp.dot(normed_cast, w_gout, preferred_element_type=jnp.float32)
    gate_sig = jax.nn.sigmoid(gate_pre)
    gout = jax.nn.sigmoid(gout_pre)
    operands = (projected * gate_sig * cell_mask).astype(jnp.bfloat16)
    left_ch, right_ch = (
        lax.all_to_all(operands[..., :width], "ch", split_axis=2, concat_axis=1, tiled=True),
        lax.all_to_all(operands[..., width:], "ch", split_axis=2, concat_axis=1, tiled=True),
    )

    def add_tri(carry, piece, start):
        update = jnp.einsum("ikc,jkc->ijc", left_ch, piece, preferred_element_type=jnp.float32)
        return update

    tri_sum = fold_right(right_ch, add_tri, jnp.zeros(left_ch.shape, jnp.float32))
    tri_cast = tri_sum.astype(jnp.bfloat16)
    tri_cells = lax.all_to_all(tri_cast, "ch", split_axis=1, concat_axis=2, tiled=True)
    outnorm, back_out = jax.vjp(
        lambda field: norm_affine(field, gain_out, bias_out), tri_cells.astype(jnp.float32)
    )
    outnorm_cast = outnorm.astype(jnp.bfloat16)
    out_lin = jnp.dot(outnorm_cast, w_out, preferred_element_type=jnp.float32)
    new_pair = (pair + out_lin * gout).astype(jnp.bfloat16)
    swapped = lax.all_to_all(
        lax.all_to_all(new_pair, "ch", split_axis=2, concat_axis=1, tiled=True),
        ("blk", "sub"),
        split_axis=1,
        concat_axis=0,
        tiled=True,
    )
    pair_cols = jnp.transpose(swapped, (1, 0, 2))
    d_new = cotangent.astype(jnp.float32)
    d_lin = d_new * gout
    d_gout_pre = d_new * out_lin * gout * (1.0 - gout)
    local_w_out = flat_grad(outnorm_cast, d_lin, width, width)
    d_norm = jnp.dot(d_lin, w_out.astype(jnp.float32).T, precision=lax.Precision.HIGHEST)
    (d_tri,) = back_out(d_norm)
    d_tri_cast = d_tri.astype(jnp.bfloat16)
    d_tri_ch = lax.all_to_all(d_tri_cast, "ch", split_axis=2, concat_axis=1, tiled=True)

    def add_left(carry, piece, start):
        return jnp.einsum("ijc,jkc->ikc", d_tri_ch, piece, preferred_element_type=jnp.float32)

    d_left = fold_right(right_ch, add_left, jnp.zeros(left_ch.shape, jnp.float32))
    d_tri_swap = lax.all_to_all(d_tri_ch, ("blk", "sub"), split_axis=1, concat_axis=0, tiled=True)
    d_right = jnp.einsum(
        "ijc,ikc->jkc",
        d_tri_swap,
        lax.all_gather(left_ch, ("blk", "sub"), axis=0, tiled=True),
        preferred_element_type=jnp.float32,
    )
    back_left, back_right = (
        lax.all_to_all(d_left.astype(jnp.bfloat16), "ch", split_axis=1, concat_axis=2, tiled=True),
        lax.all_to_all(d_right.astype(jnp.bfloat16), "ch", split_axis=1, concat_axis=2, tiled=True),
    )
    d_operands = jnp.concatenate([back_left, back_right], axis=-1).astype(jnp.float32)
    d_proj = d_operands * gate_sig * cell_mask
    d_gate = d_operands * projected * gate_sig * (1.0 - gate_sig) * cell_mask
    local_w_proj = flat_grad(normed_cast, d_proj, width, 2 * width)
    local_w_gate = flat_grad(normed_cast, d_gate, width, 2 * width)
    local_w_gout = flat_grad(normed_cast, d_gout_pre, width, width)
    highest = lax.Precision.HIGHEST
    d_normed = jnp.dot(d_proj, w_proj.astype(jnp.float32).T, precision=highest)
    d_normed = d_normed + jnp.dot(d_gate, w_gate.astype(jnp.float32).T, precision=highest)
    d_normed = d_normed + jnp.dot(d_gout_pre, w_gout.astype(jnp.float32).T, precision=highest)
    (d_pair,) = back_in(d_normed)
    grad_pair = d_new + d_pair
    grad_w_proj, grad_w_gate, grad_w_gout, grad_w_out = lax.psum(
        (local_w_proj, local_w_gate, local_w_gout, local_w_out), ("blk", "ch", "sub")
    )
    return (new_pair, pair_cols, grad_pair, grad_w_proj, grad_w_gate, grad_w_gout, grad_w_out)


most_vmem = (64 << 20) - (96 << 10)

OPS, TRI, DTRI, DOPS, RS_A, AG_A, RS_B, AG_B, PHASES = range(9)


def column_norm(field):
    mean = jnp.mean(field, axis=0, keepdims=True)
    centred = field - mean
    spread = jnp.mean(centred * centred, axis=0, keepdims=True)
    scale = lax.rsqrt(spread + eps)
    return centred * scale, scale


def column_norm_back(unit, scale, d_unit):
    first = jnp.mean(d_unit, axis=0, keepdims=True)
    second = jnp.mean(d_unit * unit, axis=0, keepdims=True)
    return scale * (d_unit - first - unit * second)


def matmul(a, b, dims=((1,), (0,))):
    return lax.dot_general(a, b, (dims, ((), ())), preferred_element_type=jnp.float32)


def low(x):
    return x.astype(jnp.bfloat16)


def wide(x):
    return x.astype(jnp.float32)


def kernel(
    sizes,
    rows,
    cols,
    live_ref,
    *refs,
):
    inputs, outputs, scratch = refs[:12], refs[12:19], refs[19:]
    loaded, made, scratch = scratch[:12], scratch[12:19], scratch[19:]
    (
    pair_ref,
    cot_ref,
    chain_ref,
    embed_ref,
    gain_in_ref,
    bias_in_ref,
    gain_out_ref,
    bias_out_ref,
    w_proj_ref,
    w_gate_ref,
    w_gout_ref,
    w_out_ref,
    ) = loaded
    (
    new_ref,
    swapped_ref,
    grad_ref,
    g_proj_ref,
    g_gate_ref,
    g_gout_ref,
    g_out_ref,
    ) = made
    (
    s_ops, r_ops, s_tri, r_tri, s_dtri, r_dtri, s_dops, r_dops,
    s_rsa, r_rsa, s_aga, r_aga, s_rsb, r_rsb, s_agb, r_agb,
    s_col, r_col,
    pair_buf, normed_buf, proj_buf, gate_buf, gout_buf, dlin_buf, dnew_buf, dgout_buf,
    pairs16, pairs8, left_buf, right_buf, flat16, flat8, cells_buf, rows_buf, col_f32, swap_f32,
    send_sem, recv_sem, col_send, col_recv, load_sem, store_sem,
    ) = scratch
    nblk, nsub, nch = sizes["blk"], sizes["sub"], sizes["ch"]
    n = nblk * nsub * nch
    width = pair_ref.shape[1]
    per = width // n
    cells = rows * cols
    half = cells // 2
    half_rows = rows // 2
    tokens = cols * nch
    my_row = lax.axis_index("blk") * nsub + lax.axis_index("sub")
    my_ch = lax.axis_index("ch")
    me = my_row * nch + my_ch

    def place(row, col):
        return {"blk": row // nsub, "sub": row % nsub, "ch": col}

    def partner(t):
        q, bit = me, 1
        while bit <= t:
            if t & bit:
                q = q + bit * (1 - 2 * (me // bit % 2))
            bit *= 2
        return q

    def start(phase, src_of, dst):
        copies = []
        for t in reversed(range(1, n)):
            q = partner(t)
            copy = pltpu.make_async_remote_copy(
                src_ref=src_of(q),
                dst_ref=dst.at[me],
                send_sem=send_sem.at[phase, t],
                recv_sem=recv_sem.at[phase, t],
                device_id=place(q // nch, q % nch),
                device_id_type=pl.DeviceIdType.MESH,
            )
            copy.start()
            copies.append(copy)
        return copies

    def arrive(phase, copies, dst):
        for t in range(1, n):
            q = partner(t)
            pltpu.make_async_remote_copy(
                src_ref=dst.at[q],
                dst_ref=dst.at[q],
                send_sem=send_sem.at[phase, t],
                recv_sem=recv_sem.at[phase, t],
                device_id=place(q // nch, q % nch),
                device_id_type=pl.DeviceIdType.MESH,
            ).wait_recv()

    sent = []

    def store(q):
        pltpu.make_async_copy(made[q], outputs[q], store_sem.at[q]).start()

    def exchange(phase, src, dst):
        sent.extend(start(phase, lambda q: src.at[q], dst))
        dst[me] = src[me]

    barrier = pltpu.get_barrier_semaphore()
    for t in range(1, n):
        q = partner(t)
        pl.semaphore_signal(
            barrier,
            inc=1,
            device_id=place(q // nch, q % nch),
            device_id_type=pl.DeviceIdType.MESH,
        )

    loads = [
        pltpu.make_async_copy(inputs[q], loaded[q], load_sem.at[q]) for q in range(12)
    ]
    for load in loads:
        load.start()
    for load in loads:
        load.wait()

    vectors = jnp.concatenate(
        [
            embed_ref[...],
            gain_in_ref[...],
            bias_in_ref[...],
            gain_out_ref[...],
            bias_out_ref[...],
            jnp.zeros((3, width), jnp.float32),
        ],
        axis=0,
    ).T
    embed, gain_in, bias_in, gain_out, bias_out = [vectors[:, q : q + 1] for q in range(5)]

    cell = lax.broadcasted_iota(jnp.int32, (tokens, cells), 1)
    token = lax.broadcasted_iota(jnp.int32, (tokens, cells), 0)
    local_row = jnp.zeros((tokens, cells), jnp.int32)
    for q in range(1, rows):
        local_row = local_row + (cell >= q * cols).astype(jnp.int32)
    row_pos = my_row * rows + local_row
    col_pos = my_ch * cols + cell - local_row * cols
    pick = (token == row_pos).astype(jnp.float32) - (token == col_pos).astype(jnp.float32)
    chain = jnp.broadcast_to(wide(chain_ref[...]), (8, tokens))
    apart = matmul(low(chain), low(pick))[0:1]
    same = (apart == 0.0).astype(jnp.float32)
    length = live_ref[0, 0]
    mask = (row_pos[0:1] < length).astype(jnp.float32) * (col_pos[0:1] < length).astype(jnp.float32)

    pair = wide(pair_ref[...]).T + same * embed
    pair_buf[...] = pair
    unit_in, scale_in = column_norm(pair)
    normed = low(unit_in * gain_in + bias_in)
    normed_buf[...] = normed
    projected = matmul(low(wide(w_proj_ref[...]).T), normed)
    gate_sig = jax.nn.sigmoid(matmul(low(wide(w_gate_ref[...]).T), normed))
    masked = gate_sig * mask
    operands = projected * masked
    gate_buf[...] = masked
    proj_buf[...] = operands * (1.0 - gate_sig)
    for q in range(n):
        low_q, high_q = q * per, width + q * per
        s_ops[q] = low(
            jnp.concatenate(
                [operands[low_q : low_q + per], operands[high_q : high_q + per]], axis=0
            )
        )
    pl.semaphore_wait(barrier, n - 1)
    exchange(OPS, s_ops, r_ops)

    gout = jax.nn.sigmoid(matmul(low(wide(w_gout_ref[...]).T), normed))
    gout_buf[...] = gout
    d_new = wide(cot_ref[...]).T
    dnew_buf[...] = d_new
    d_lin = low(d_new * gout)
    dlin_buf[...] = d_lin
    d_unit_out = matmul(w_out_ref[...], d_lin) * gain_out
    w_out_t = low(wide(w_out_ref[...]).T)

    arrive(OPS, None, r_ops)
    for q in range(n):
        block_row, block_col = q // nch, q % nch
        x = wide(r_ops[q])
        for i in range(rows):
            at = (block_row * rows + i) * 2 * per
            pairs16[at : at + 2 * per, block_col * cols : (block_col + 1) * cols] = x[
                :, i * cols : (i + 1) * cols
            ]
    for c in range(per):
        left = low(pairs16[pl.ds(c, tokens, stride=2 * per), :])
        right = low(pairs16[pl.ds(per + c, tokens, stride=2 * per), :])
        left_buf[c] = left
        right_buf[c] = right
        pairs8[pl.ds(c, tokens, stride=per), :] = matmul(left, right, ((1,), (1,)))
    for q in range(n):
        block_row, block_col = q // nch, q % nch
        for i in range(rows):
            at = (block_row * rows + i) * per
            down, along = (i // half_rows) * per, (i % half_rows) * cols
            flat8[q, down : down + per, along : along + cols] = pairs8[
                at : at + per, block_col * cols : (block_col + 1) * cols
            ]
        s_tri[q] = low(flat8[q])
    exchange(TRI, s_tri, r_tri)
    arrive(TRI, None, r_tri)
    for q in range(n):
        x = wide(r_tri[q])
        cells_buf[q * per : (q + 1) * per, 0:half] = x[0:per]
        cells_buf[q * per : (q + 1) * per, half:cells] = x[per : 2 * per]

    unit_out, scale_out = column_norm(cells_buf[...])
    d_tri = column_norm_back(unit_out, scale_out, d_unit_out)
    for q in range(n):
        x = d_tri[q * per : (q + 1) * per]
        s_dtri[q] = low(jnp.concatenate([x[:, 0:half], x[:, half:cells]], axis=0))
    exchange(DTRI, s_dtri, r_dtri)

    outnorm = low(unit_out * gain_out + bias_out)
    out_lin = matmul(w_out_t, outnorm)
    gout = gout_buf[...]
    moved = out_lin * gout
    d_gout = low(dnew_buf[...] * moved * (1.0 - gout))
    dgout_buf[...] = d_gout
    grad_gout = matmul(normed_buf[...], d_gout, ((1,), (1,)))
    grad_out = matmul(outnorm, dlin_buf[...], ((1,), (1,)))
    for q in range(n):
        at = q * per
        s_rsa[q] = low(
            jnp.concatenate([grad_gout[at : at + per], grad_out[at : at + per]], axis=0)
        )
    exchange(RS_A, s_rsa, r_rsa)

    rows_buf[...] = (pair_buf[...] + moved).T
    new_ref[...] = low(rows_buf[...])
    store(0)
    share = cols // rows
    lanes = width // nch
    first = lax.broadcasted_iota(jnp.int32, (rows, width), 1) < lanes
    for m in range(share):
        for j in range(half_rows):
            a = rows_buf[pl.ds(m * rows + j, rows, stride=cols), :]
            b = rows_buf[pl.ds(m * rows + j + half_rows, rows, stride=cols), :]
            col_f32[m * nch, j * rows : (j + 1) * rows, :] = jnp.where(
                first, a, pltpu.roll(b, lanes, 1)
            )
            col_f32[m * nch + 1, j * rows : (j + 1) * rows, :] = jnp.where(
                first, pltpu.roll(a, lanes, 1), b
            )
        for col in range(nch):
            used = half_rows * rows
            spare = col_f32.shape[1] - used
            if spare:
                col_f32[m * nch + col, used : used + spare, :] = jnp.zeros(
                    (spare, width), jnp.float32
                )
            s_col[m * nch + col] = low(col_f32[m * nch + col])

    def col_copy(slot, row, col):
        return pltpu.make_async_remote_copy(
            src_ref=s_col.at[slot],
            dst_ref=r_col.at[my_row],
            send_sem=col_send.at[slot],
            recv_sem=col_recv.at[my_row],
            device_id=place(row, col),
            device_id_type=pl.DeviceIdType.MESH,
        )

    for m in range(share):
        for col in range(nch):
            slot = m * nch + col
            row = my_ch * share + m
            here = row * nch + col == me

            @pl.when(here)
            def _():
                r_col[my_row] = s_col[slot]

            @pl.when(jnp.logical_not(here))
            def _():
                col_copy(slot, row, col).start()

    arrive(DTRI, None, r_dtri)
    for q in range(n):
        block_row, block_col = q // nch, q % nch
        x = wide(r_dtri[q])
        for i in range(rows):
            at = (block_row * rows + i) * per
            down, along = (i // half_rows) * per, (i % half_rows) * cols
            pairs8[at : at + per, block_col * cols : (block_col + 1) * cols] = x[
                down : down + per, along : along + cols
            ]
    for c in range(per):
        grad = pairs8[pl.ds(c, tokens, stride=per), :]
        pairs16[pl.ds(c, tokens, stride=2 * per), :] = matmul(low(grad), right_buf[c])
        pairs16[pl.ds(per + c, tokens, stride=2 * per), :] = matmul(low(grad.T), left_buf[c])
    for q in range(n):
        block_row, block_col = q // nch, q % nch
        for i in range(rows):
            at = (block_row * rows + i) * 2 * per
            flat16[q, :, i * cols : (i + 1) * cols] = pairs16[
                at : at + 2 * per, block_col * cols : (block_col + 1) * cols
            ]
        s_dops[q] = low(flat16[q])
    exchange(DOPS, s_dops, r_dops)

    def summed(buf):
        total = wide(buf[0])
        for q in range(1, n):
            total = total + wide(buf[q])
        return low(total)

    arrive(RS_A, None, r_rsa)
    s_aga[...] = summed(r_rsa)
    sent.extend(start(AG_A, lambda q: s_aga, r_aga))
    r_aga[me] = s_aga[...]

    for row in range(nblk * nsub):
        source = row * nch + my_row // share

        @pl.when(source != me)
        def _():
            pltpu.make_async_remote_copy(
                src_ref=r_col.at[row],
                dst_ref=r_col.at[row],
                send_sem=col_send.at[0],
                recv_sem=col_recv.at[row],
                device_id=place(row, my_row // share),
                device_id_type=pl.DeviceIdType.MESH,
            ).wait_recv()

        for j in range(half_rows):
            x = wide(r_col[row])[j * rows : (j + 1) * rows]
            swap_f32[j, row * rows : (row + 1) * rows, :] = x[:, 0:lanes]
            swap_f32[j + half_rows, row * rows : (row + 1) * rows, :] = x[:, lanes:width]
    for j in range(rows):
        swapped_ref[j] = low(swap_f32[j].T)
    store(1)
    d_normed_gout = matmul(w_gout_ref[...], dgout_buf[...])

    arrive(DOPS, None, r_dops)
    d_operands = jnp.concatenate(
        [wide(r_dops[q])[0:per] for q in range(n)]
        + [wide(r_dops[q])[per : 2 * per] for q in range(n)],
        axis=0,
    )
    d_proj = low(d_operands * gate_buf[...])
    d_gate = low(d_operands * proj_buf[...])
    normed = normed_buf[...]
    grad_proj = matmul(normed, d_proj, ((1,), (1,)))
    grad_gate = matmul(normed, d_gate, ((1,), (1,)))
    for q in range(n):
        at = q * per
        s_rsb[q] = low(
            jnp.concatenate([grad_proj[at : at + per], grad_gate[at : at + per]], axis=0)
        )
    exchange(RS_B, s_rsb, r_rsb)

    d_normed = d_normed_gout + matmul(w_proj_ref[...], d_proj) + matmul(w_gate_ref[...], d_gate)
    unit_in, scale_in = column_norm(pair_buf[...])
    d_pair = column_norm_back(unit_in, scale_in, d_normed * gain_in)
    total = dnew_buf[...] + d_pair

    arrive(RS_B, None, r_rsb)
    s_agb[...] = summed(r_rsb)
    sent.extend(start(AG_B, lambda q: s_agb, r_agb))
    r_agb[me] = s_agb[...]
    grad_ref[...] = total.T
    store(2)
    arrive(AG_A, None, r_aga)
    for q in range(n):
        x = wide(r_aga[q])
        g_gout_ref[q * per : (q + 1) * per, :] = x[0:per]
        g_out_ref[q * per : (q + 1) * per, :] = x[per : 2 * per]
    store(5)
    store(6)
    arrive(AG_B, None, r_agb)
    for q in range(n):
        x = wide(r_agb[q])
        g_proj_ref[q * per : (q + 1) * per, :] = x[0:per]
        g_gate_ref[q * per : (q + 1) * per, :] = x[per : 2 * per]

    store(3)
    store(4)
    for copy in sent:
        copy.wait_send()
    for m in range(share):
        for col in range(nch):
            slot = m * nch + col
            row = my_ch * share + m

            @pl.when(row * nch + col != me)
            def _():
                col_copy(slot, row, col).wait_send()

    for q in range(7):
        pltpu.make_async_copy(made[q], outputs[q], store_sem.at[q]).wait()


def write_kernel(*refs):
    count = len(refs) // 2
    copies = [
        pltpu.make_async_copy(refs[q], refs[count + q], refs[-1].at[q]) for q in range(count)
    ]
    for copy in copies:
        copy.start()
    for copy in copies:
        copy.wait()


def write_out(values):
    return pl.pallas_call(
        write_kernel,
        out_shape=tuple(jax.ShapeDtypeStruct(x.shape, x.dtype) for x in values),
        in_specs=[pl.BlockSpec(memory_space=pltpu.HBM)] * len(values),
        out_specs=[pl.BlockSpec(memory_space=pltpu.HBM)] * len(values),
        scratch_shapes=[pltpu.SemaphoreType.DMA((len(values),))],
        compiler_params=pltpu.CompilerParams(vmem_limit_bytes=most_vmem),
    )(*values)


def fused(
    sizes,
    pair_in,
    cotangent,
    chain_ids,
    live_length,
    chain_embed,
    gain_in,
    bias_in,
    w_proj,
    w_gate,
    w_gout,
    gain_out,
    bias_out,
    w_out,
):
    rows, cols, width = pair_in.shape
    n = sizes["blk"] * sizes["sub"] * sizes["ch"]
    per = width // n
    cells, tokens, lanes = rows * cols, cols * sizes["ch"], width // sizes["ch"]
    half = cells // 2
    slots = cols // rows * sizes["ch"]
    col_rows = -(-(rows // 2 * rows) // 16) * 16
    bf, f32 = jnp.bfloat16, jnp.float32
    vm = pltpu.VMEM

    def both(*shape):
        return [vm((n,) + shape, bf), vm((n,) + shape, bf)]

    line = lambda x: x.reshape(1, -1)
    operands = (
        pair_in.reshape(cells, width),
        cotangent.reshape(cells, width),
        line(chain_ids),
        line(chain_embed),
        line(gain_in),
        line(bias_in),
        line(gain_out),
        line(bias_out),
        w_proj,
        w_gate,
        w_gout,
        w_out,
    )
    results = (
        jax.ShapeDtypeStruct((cells, width), bf),
        jax.ShapeDtypeStruct((rows, lanes, tokens), bf),
        jax.ShapeDtypeStruct((cells, width), f32),
        jax.ShapeDtypeStruct((width, 2 * width), f32),
        jax.ShapeDtypeStruct((width, 2 * width), f32),
        jax.ShapeDtypeStruct((width, width), f32),
        jax.ShapeDtypeStruct((width, width), f32),
    )
    outs = pl.pallas_call(
        functools.partial(kernel, sizes, rows, cols),
        out_shape=results,
        in_specs=[pl.BlockSpec(memory_space=pltpu.SMEM)]
        + [pl.BlockSpec(memory_space=pltpu.HBM)] * 12,
        out_specs=[pl.BlockSpec(memory_space=pltpu.HBM)] * 7,
        scratch_shapes=[vm(x.shape, x.dtype) for x in operands + results]
        + both(2 * per, cells)
        + both(2 * per, half)
        + both(2 * per, half)
        + both(2 * per, cells)
        + both(2 * per, width)
        + [vm((2 * per, width), bf), vm((n, 2 * per, width), bf)]
        + both(2 * per, 2 * width)
        + [vm((2 * per, 2 * width), bf), vm((n, 2 * per, 2 * width), bf)]
        + [vm((slots, col_rows, width), bf), vm((n // sizes["ch"], col_rows, width), bf)]
        + [
            vm((width, cells), f32),
            vm((width, cells), bf),
            vm((2 * width, cells), f32),
            vm((2 * width, cells), f32),
            vm((width, cells), f32),
            vm((width, cells), bf),
            vm((width, cells), f32),
            vm((width, cells), bf),
            vm((tokens * 2 * per, tokens), f32),
            vm((tokens * per, tokens), f32),
            vm((per, tokens, tokens), bf),
            vm((per, tokens, tokens), bf),
            vm((n, 2 * per, cells), f32),
            vm((n, 2 * per, half), f32),
            vm((width, cells), f32),
            vm((cells, width), f32),
            vm((slots, col_rows, width), f32),
            vm((rows, tokens, lanes), f32),
            pltpu.SemaphoreType.DMA((PHASES, n)),
            pltpu.SemaphoreType.DMA((PHASES, n)),
            pltpu.SemaphoreType.DMA((slots,)),
            pltpu.SemaphoreType.DMA((n // sizes["ch"],)),
            pltpu.SemaphoreType.DMA((12,)),
            pltpu.SemaphoreType.DMA((7,)),
        ],
        compiler_params=pltpu.CompilerParams(
            collective_id=0, has_side_effects=True, vmem_limit_bytes=most_vmem
        ),
    )(line(live_length), *operands)
    outs = write_out(outs)
    new_pair, pair_cols, grad_pair, *grads = outs
    return (
        new_pair.reshape(rows, cols, width),
        jnp.swapaxes(pair_cols, 1, 2),
        grad_pair.reshape(rows, cols, width),
        *grads,
    )


def solution(mesh):
    sizes = dict(mesh.shape)
    devices = sizes["blk"] * sizes["sub"] * sizes["ch"]
    fits = devices * 8 == 128 and sizes["ch"] == 2
    body = functools.partial(fused, sizes) if fits else on_device
    return jax.shard_map(
        body,
        mesh=mesh,
        in_specs=(
            P(("grp", "blk", "sub"), "ch", None),
            P(("grp", "blk", "sub"), "ch", None),
            P("grp"),
            P("grp"),
            P(),
            P(),
            P(),
            P(),
            P(),
            P(),
            P(),
            P(),
            P(),
        ),
        out_specs=(
            P(("grp", "blk", "sub"), "ch", None),
            P(("grp", "blk", "sub"), None, "ch"),
            P(("grp", "blk", "sub"), "ch", None),
            P("grp", None),
            P("grp", None),
            P("grp", None),
            P("grp", None),
        ),
        check_vma=False,
    )
```

```python
import functools

import jax
import jax.numpy as jnp
from jax import lax
from jax.experimental import pallas as pl
from jax.experimental.pallas import tpu as pltpu
from jax.sharding import PartitionSpec as P

eps = 1e-05


def norm_affine(field, gain, bias):
    mean = jnp.mean(field, axis=-1, keepdims=True)
    centred = field - mean
    spread = jnp.mean(centred * centred, axis=-1, keepdims=True)
    return centred * lax.rsqrt(spread + eps) * gain + bias


def flat_grad(left_cells, right_cells, width_left, width_right):
    left_flat = left_cells.reshape(-1, width_left)
    right_flat = right_cells.reshape(-1, width_right)
    right_high = right_flat.astype(jnp.bfloat16)
    right_low = (right_flat - right_high.astype(jnp.float32)).astype(jnp.bfloat16)
    dims = (((0,), (0,)), ((), ()))
    upper = lax.dot_general(left_flat, right_high, dims, preferred_element_type=jnp.float32)
    lower = lax.dot_general(left_flat, right_low, dims, preferred_element_type=jnp.float32)
    return upper + lower


def fold_right(right_ch, update, initial):
    return update(
        initial, lax.all_gather(right_ch, ("blk", "sub"), axis=0, tiled=True), jnp.int32(0)
    )


def on_device(
    pair_in,
    cotangent,
    chain_ids,
    live_length,
    chain_embed,
    gain_in,
    bias_in,
    w_proj,
    w_gate,
    w_gout,
    gain_out,
    bias_out,
    w_out,
):
    row_count = pair_in.shape[0]
    col_count = pair_in.shape[1]
    width = pair_in.shape[2]
    row_start = lax.axis_index(("blk", "sub")) * row_count
    col_start = lax.axis_index("ch") * col_count
    row_pos = row_start + jnp.arange(row_count, dtype=jnp.int32)
    col_pos = col_start + jnp.arange(col_count, dtype=jnp.int32)
    live_rows = (row_pos < live_length[0]).astype(jnp.float32)
    live_cols = (col_pos < live_length[0]).astype(jnp.float32)
    cell_mask = (live_rows[:, None] * live_cols[None, :])[..., None]
    chain_rows = lax.dynamic_slice_in_dim(chain_ids, row_start, row_count)
    chain_cols = lax.dynamic_slice_in_dim(chain_ids, col_start, col_count)
    same = (chain_rows[:, None] == chain_cols[None, :]).astype(jnp.float32)
    pair = pair_in.astype(jnp.float32) + same[..., None] * chain_embed
    normed, back_in = jax.vjp(lambda field: norm_affine(field, gain_in, bias_in), pair)
    normed_cast = normed.astype(jnp.bfloat16)
    projected = jnp.dot(normed_cast, w_proj, preferred_element_type=jnp.float32)
    gate_pre = jnp.dot(normed_cast, w_gate, preferred_element_type=jnp.float32)
    gout_pre = jnp.dot(normed_cast, w_gout, preferred_element_type=jnp.float32)
    gate_sig = jax.nn.sigmoid(gate_pre)
    gout = jax.nn.sigmoid(gout_pre)
    operands = (projected * gate_sig * cell_mask).astype(jnp.bfloat16)
    left_ch, right_ch = (
        lax.all_to_all(operands[..., :width], "ch", split_axis=2, concat_axis=1, tiled=True),
        lax.all_to_all(operands[..., width:], "ch", split_axis=2, concat_axis=1, tiled=True),
    )

    def add_tri(carry, piece, start):
        update = jnp.einsum("ikc,jkc->ijc", left_ch, piece, preferred_element_type=jnp.float32)
        return update

    tri_sum = fold_right(right_ch, add_tri, jnp.zeros(left_ch.shape, jnp.float32))
    tri_cast = tri_sum.astype(jnp.bfloat16)
    tri_cells = lax.all_to_all(tri_cast, "ch", split_axis=1, concat_axis=2, tiled=True)
    outnorm, back_out = jax.vjp(
        lambda field: norm_affine(field, gain_out, bias_out), tri_cells.astype(jnp.float32)
    )
    outnorm_cast = outnorm.astype(jnp.bfloat16)
    out_lin = jnp.dot(outnorm_cast, w_out, preferred_element_type=jnp.float32)
    new_pair = (pair + out_lin * gout).astype(jnp.bfloat16)
    swapped = lax.all_to_all(
        lax.all_to_all(new_pair, "ch", split_axis=2, concat_axis=1, tiled=True),
        ("blk", "sub"),
        split_axis=1,
        concat_axis=0,
        tiled=True,
    )
    pair_cols = jnp.transpose(swapped, (1, 0, 2))
    d_new = cotangent.astype(jnp.float32)
    d_lin = d_new * gout
    d_gout_pre = d_new * out_lin * gout * (1.0 - gout)
    local_w_out = flat_grad(outnorm_cast, d_lin, width, width)
    d_norm = jnp.dot(d_lin, w_out.astype(jnp.float32).T, precision=lax.Precision.HIGHEST)
    (d_tri,) = back_out(d_norm)
    d_tri_cast = d_tri.astype(jnp.bfloat16)
    d_tri_ch = lax.all_to_all(d_tri_cast, "ch", split_axis=2, concat_axis=1, tiled=True)

    def add_left(carry, piece, start):
        return jnp.einsum("ijc,jkc->ikc", d_tri_ch, piece, preferred_element_type=jnp.float32)

    d_left = fold_right(right_ch, add_left, jnp.zeros(left_ch.shape, jnp.float32))
    d_tri_swap = lax.all_to_all(d_tri_ch, ("blk", "sub"), split_axis=1, concat_axis=0, tiled=True)
    d_right = jnp.einsum(
        "ijc,ikc->jkc",
        d_tri_swap,
        lax.all_gather(left_ch, ("blk", "sub"), axis=0, tiled=True),
        preferred_element_type=jnp.float32,
    )
    back_left, back_right = (
        lax.all_to_all(d_left.astype(jnp.bfloat16), "ch", split_axis=1, concat_axis=2, tiled=True),
        lax.all_to_all(d_right.astype(jnp.bfloat16), "ch", split_axis=1, concat_axis=2, tiled=True),
    )
    d_operands = jnp.concatenate([back_left, back_right], axis=-1).astype(jnp.float32)
    d_proj = d_operands * gate_sig * cell_mask
    d_gate = d_operands * projected * gate_sig * (1.0 - gate_sig) * cell_mask
    local_w_proj = flat_grad(normed_cast, d_proj, width, 2 * width)
    local_w_gate = flat_grad(normed_cast, d_gate, width, 2 * width)
    local_w_gout = flat_grad(normed_cast, d_gout_pre, width, width)
    highest = lax.Precision.HIGHEST
    d_normed = jnp.dot(d_proj, w_proj.astype(jnp.float32).T, precision=highest)
    d_normed = d_normed + jnp.dot(d_gate, w_gate.astype(jnp.float32).T, precision=highest)
    d_normed = d_normed + jnp.dot(d_gout_pre, w_gout.astype(jnp.float32).T, precision=highest)
    (d_pair,) = back_in(d_normed)
    grad_pair = d_new + d_pair
    grad_w_proj, grad_w_gate, grad_w_gout, grad_w_out = lax.psum(
        (local_w_proj, local_w_gate, local_w_gout, local_w_out), ("blk", "ch", "sub")
    )
    return (new_pair, pair_cols, grad_pair, grad_w_proj, grad_w_gate, grad_w_gout, grad_w_out)


most_vmem = (64 << 20) - (96 << 10)

OPS, TRI, DTRI, DOPS, RS_A, RS_B, AG_B, PHASES = range(8)


def column_norm(field):
    mean = jnp.mean(field, axis=0, keepdims=True)
    centred = field - mean
    spread = jnp.mean(centred * centred, axis=0, keepdims=True)
    scale = lax.rsqrt(spread + eps)
    return centred * scale, scale


def column_norm_back(unit, scale, d_unit):
    first = jnp.mean(d_unit, axis=0, keepdims=True)
    second = jnp.mean(d_unit * unit, axis=0, keepdims=True)
    return scale * (d_unit - first - unit * second)


def matmul(a, b, dims=((1,), (0,))):
    return lax.dot_general(a, b, (dims, ((), ())), preferred_element_type=jnp.float32)


def low(x):
    return x.astype(jnp.bfloat16)


def wide(x):
    return x.astype(jnp.float32)


def kernel(
    sizes,
    rows,
    cols,
    live_ref,
    *refs,
):
    inputs, outputs, scratch = refs[:12], refs[12:19], refs[19:]
    loaded, made, scratch = scratch[:12], scratch[12:19], scratch[19:]
    (
    pair_ref,
    cot_ref,
    chain_ref,
    embed_ref,
    gain_in_ref,
    bias_in_ref,
    gain_out_ref,
    bias_out_ref,
    w_proj_ref,
    w_gate_ref,
    w_gout_ref,
    w_out_ref,
    ) = loaded
    (
    new_ref,
    swapped_ref,
    grad_ref,
    g_proj_ref,
    g_gate_ref,
    g_gout_ref,
    g_out_ref,
    ) = made
    (
    s_ops, r_ops, s_tri, r_tri, s_dtri, r_dtri, s_dops, r_dops,
    s_rsa, r_rsa, s_rsb, r_rsb, s_agb, r_agb,
    s_col, r_col,
    pair_buf, normed_buf, proj_buf, gate_buf, gout_buf, dlin_buf, dnew_buf, dgout_buf,
    pairs16, pairs8, left_buf, right_buf, flat16, flat8, cells_buf, rows_buf, col_f32, swap_f32,
    send_sem, recv_sem, col_send, col_recv, load_sem, store_sem,
    ) = scratch
    nblk, nsub, nch = sizes["blk"], sizes["sub"], sizes["ch"]
    n = nblk * nsub * nch
    width = pair_ref.shape[1]
    per = width // n
    cells = rows * cols
    half = cells // 2
    half_rows = rows // 2
    tokens = cols * nch
    my_row = lax.axis_index("blk") * nsub + lax.axis_index("sub")
    my_ch = lax.axis_index("ch")
    me = my_row * nch + my_ch

    def place(row, col):
        return {"blk": row // nsub, "sub": row % nsub, "ch": col}

    def partner(t):
        q, bit = me, 1
        while bit <= t:
            if t & bit:
                q = q + bit * (1 - 2 * (me // bit % 2))
            bit *= 2
        return q

    def start(phase, src_of, dst):
        copies = []
        for t in reversed(range(1, n)):
            q = partner(t)
            copy = pltpu.make_async_remote_copy(
                src_ref=src_of(q),
                dst_ref=dst.at[me],
                send_sem=send_sem.at[phase, t],
                recv_sem=recv_sem.at[phase, t],
                device_id=place(q // nch, q % nch),
                device_id_type=pl.DeviceIdType.MESH,
            )
            copy.start()
            copies.append(copy)
        return copies

    def arrive(phase, copies, dst):
        for t in range(1, n):
            q = partner(t)
            pltpu.make_async_remote_copy(
                src_ref=dst.at[q],
                dst_ref=dst.at[q],
                send_sem=send_sem.at[phase, t],
                recv_sem=recv_sem.at[phase, t],
                device_id=place(q // nch, q % nch),
                device_id_type=pl.DeviceIdType.MESH,
            ).wait_recv()

    sent = []

    def store(q):
        pltpu.make_async_copy(made[q], outputs[q], store_sem.at[q]).start()

    def exchange(phase, src, dst):
        sent.extend(start(phase, lambda q: src.at[q], dst))
        dst[me] = src[me]

    barrier = pltpu.get_barrier_semaphore()
    for t in range(1, n):
        q = partner(t)
        pl.semaphore_signal(
            barrier,
            inc=1,
            device_id=place(q // nch, q % nch),
            device_id_type=pl.DeviceIdType.MESH,
        )

    loads = [
        pltpu.make_async_copy(inputs[q], loaded[q], load_sem.at[q]) for q in range(12)
    ]
    for load in loads:
        load.start()
    for load in loads:
        load.wait()

    vectors = jnp.concatenate(
        [
            embed_ref[...],
            gain_in_ref[...],
            bias_in_ref[...],
            gain_out_ref[...],
            bias_out_ref[...],
            jnp.zeros((3, width), jnp.float32),
        ],
        axis=0,
    ).T
    embed, gain_in, bias_in, gain_out, bias_out = [vectors[:, q : q + 1] for q in range(5)]

    cell = lax.broadcasted_iota(jnp.int32, (tokens, cells), 1)
    token = lax.broadcasted_iota(jnp.int32, (tokens, cells), 0)
    local_row = jnp.zeros((tokens, cells), jnp.int32)
    for q in range(1, rows):
        local_row = local_row + (cell >= q * cols).astype(jnp.int32)
    row_pos = my_row * rows + local_row
    col_pos = my_ch * cols + cell - local_row * cols
    pick = (token == row_pos).astype(jnp.float32) - (token == col_pos).astype(jnp.float32)
    chain = jnp.broadcast_to(wide(chain_ref[...]), (8, tokens))
    apart = matmul(low(chain), low(pick))[0:1]
    same = (apart == 0.0).astype(jnp.float32)
    length = live_ref[0, 0]
    mask = (row_pos[0:1] < length).astype(jnp.float32) * (col_pos[0:1] < length).astype(jnp.float32)

    pair = wide(pair_ref[...]).T + same * embed
    pair_buf[...] = pair
    unit_in, scale_in = column_norm(pair)
    normed = low(unit_in * gain_in + bias_in)
    normed_buf[...] = normed
    projected = matmul(low(wide(w_proj_ref[...]).T), normed)
    gate_sig = jax.nn.sigmoid(matmul(low(wide(w_gate_ref[...]).T), normed))
    masked = gate_sig * mask
    operands = projected * masked
    gate_buf[...] = masked
    proj_buf[...] = operands * (1.0 - gate_sig)
    for q in range(n):
        low_q, high_q = q * per, width + q * per
        s_ops[q] = low(
            jnp.concatenate(
                [operands[low_q : low_q + per], operands[high_q : high_q + per]], axis=0
            )
        )
    pl.semaphore_wait(barrier, n - 1)
    exchange(OPS, s_ops, r_ops)

    gout = jax.nn.sigmoid(matmul(low(wide(w_gout_ref[...]).T), normed))
    gout_buf[...] = gout
    d_new = wide(cot_ref[...]).T
    dnew_buf[...] = d_new
    d_lin = low(d_new * gout)
    dlin_buf[...] = d_lin
    d_unit_out = matmul(w_out_ref[...], d_lin) * gain_out
    w_out_t = low(wide(w_out_ref[...]).T)

    arrive(OPS, None, r_ops)
    for q in range(n):
        block_row, block_col = q // nch, q % nch
        x = wide(r_ops[q])
        for i in range(rows):
            at = (block_row * rows + i) * 2 * per
            pairs16[at : at + 2 * per, block_col * cols : (block_col + 1) * cols] = x[
                :, i * cols : (i + 1) * cols
            ]
    for c in range(per):
        left = low(pairs16[pl.ds(c, tokens, stride=2 * per), :])
        right = low(pairs16[pl.ds(per + c, tokens, stride=2 * per), :])
        left_buf[c] = left
        right_buf[c] = right
        pairs8[pl.ds(c, tokens, stride=per), :] = matmul(left, right, ((1,), (1,)))
    for q in range(n):
        block_row, block_col = q // nch, q % nch
        for i in range(rows):
            at = (block_row * rows + i) * per
            down, along = (i // half_rows) * per, (i % half_rows) * cols
            flat8[q, down : down + per, along : along + cols] = pairs8[
                at : at + per, block_col * cols : (block_col + 1) * cols
            ]
        s_tri[q] = low(flat8[q])
    exchange(TRI, s_tri, r_tri)
    arrive(TRI, None, r_tri)
    for q in range(n):
        x = wide(r_tri[q])
        cells_buf[q * per : (q + 1) * per, 0:half] = x[0:per]
        cells_buf[q * per : (q + 1) * per, half:cells] = x[per : 2 * per]

    unit_out, scale_out = column_norm(cells_buf[...])
    d_tri = column_norm_back(unit_out, scale_out, d_unit_out)
    for q in range(n):
        x = d_tri[q * per : (q + 1) * per]
        s_dtri[q] = low(jnp.concatenate([x[:, 0:half], x[:, half:cells]], axis=0))
    exchange(DTRI, s_dtri, r_dtri)

    outnorm = low(unit_out * gain_out + bias_out)
    out_lin = matmul(w_out_t, outnorm)
    gout = gout_buf[...]
    moved = out_lin * gout
    d_gout = low(dnew_buf[...] * moved * (1.0 - gout))
    dgout_buf[...] = d_gout
    grad_gout = matmul(normed_buf[...], d_gout, ((1,), (1,)))
    grad_out = matmul(outnorm, dlin_buf[...], ((1,), (1,)))
    for q in range(n):
        at = q * per
        s_rsa[q] = low(
            jnp.concatenate([grad_gout[at : at + per], grad_out[at : at + per]], axis=0)
        )
    exchange(RS_A, s_rsa, r_rsa)

    rows_buf[...] = (pair_buf[...] + moved).T
    new_ref[...] = low(rows_buf[...])
    store(0)
    share = cols // rows
    lanes = width // nch
    first = lax.broadcasted_iota(jnp.int32, (rows, width), 1) < lanes
    for m in range(share):
        for j in range(half_rows):
            a = rows_buf[pl.ds(m * rows + j, rows, stride=cols), :]
            b = rows_buf[pl.ds(m * rows + j + half_rows, rows, stride=cols), :]
            col_f32[m * nch, j * rows : (j + 1) * rows, :] = jnp.where(
                first, a, pltpu.roll(b, lanes, 1)
            )
            col_f32[m * nch + 1, j * rows : (j + 1) * rows, :] = jnp.where(
                first, pltpu.roll(a, lanes, 1), b
            )
        for col in range(nch):
            used = half_rows * rows
            spare = col_f32.shape[1] - used
            if spare:
                col_f32[m * nch + col, used : used + spare, :] = jnp.zeros(
                    (spare, width), jnp.float32
                )
            s_col[m * nch + col] = low(col_f32[m * nch + col])

    def col_copy(slot, row, col):
        return pltpu.make_async_remote_copy(
            src_ref=s_col.at[slot],
            dst_ref=r_col.at[my_row],
            send_sem=col_send.at[slot],
            recv_sem=col_recv.at[my_row],
            device_id=place(row, col),
            device_id_type=pl.DeviceIdType.MESH,
        )

    for m in range(share // 2):
        for col in range(nch):
            slot = m * nch + col
            row = my_ch * share + m
            here = row * nch + col == me

            @pl.when(here)
            def _():
                r_col[my_row] = s_col[slot]

            @pl.when(jnp.logical_not(here))
            def _():
                col_copy(slot, row, col).start()

    arrive(DTRI, None, r_dtri)
    for q in range(n):
        block_row, block_col = q // nch, q % nch
        x = wide(r_dtri[q])
        for i in range(rows):
            at = (block_row * rows + i) * per
            down, along = (i // half_rows) * per, (i % half_rows) * cols
            pairs8[at : at + per, block_col * cols : (block_col + 1) * cols] = x[
                down : down + per, along : along + cols
            ]
    for c in range(per):
        grad = pairs8[pl.ds(c, tokens, stride=per), :]
        pairs16[pl.ds(c, tokens, stride=2 * per), :] = matmul(low(grad), right_buf[c])
        pairs16[pl.ds(per + c, tokens, stride=2 * per), :] = matmul(low(grad.T), left_buf[c])
    for q in range(n):
        block_row, block_col = q // nch, q % nch
        for i in range(rows):
            at = (block_row * rows + i) * 2 * per
            flat16[q, :, i * cols : (i + 1) * cols] = pairs16[
                at : at + 2 * per, block_col * cols : (block_col + 1) * cols
            ]
        s_dops[q] = low(flat16[q])
    exchange(DOPS, s_dops, r_dops)
    for m in range(share // 2, share):
        for col in range(nch):
            slot = m * nch + col
            row = my_ch * share + m
            here = row * nch + col == me

            @pl.when(here)
            def _():
                r_col[my_row] = s_col[slot]

            @pl.when(jnp.logical_not(here))
            def _():
                col_copy(slot, row, col).start()

    def summed(buf):
        total = wide(buf[0])
        for q in range(1, n):
            total = total + wide(buf[q])
        return low(total)

    d_normed_gout = matmul(w_gout_ref[...], dgout_buf[...])

    arrive(DOPS, None, r_dops)
    d_operands = jnp.concatenate(
        [wide(r_dops[q])[0:per] for q in range(n)]
        + [wide(r_dops[q])[per : 2 * per] for q in range(n)],
        axis=0,
    )
    d_proj = low(d_operands * gate_buf[...])
    d_gate = low(d_operands * proj_buf[...])
    normed = normed_buf[...]
    grad_proj = matmul(normed, d_proj, ((1,), (1,)))
    grad_gate = matmul(normed, d_gate, ((1,), (1,)))
    for q in range(n):
        at = q * per
        s_rsb[q] = low(
            jnp.concatenate([grad_proj[at : at + per], grad_gate[at : at + per]], axis=0)
        )
    exchange(RS_B, s_rsb, r_rsb)

    d_normed = d_normed_gout + matmul(w_proj_ref[...], d_proj) + matmul(w_gate_ref[...], d_gate)
    unit_in, scale_in = column_norm(pair_buf[...])
    d_pair = column_norm_back(unit_in, scale_in, d_normed * gain_in)
    total = dnew_buf[...] + d_pair

    arrive(RS_B, None, r_rsb)
    arrive(RS_A, None, r_rsa)
    s_agb[:, 0 : 2 * width] = summed(r_rsb)
    s_agb[:, 2 * width : 3 * width] = summed(r_rsa)
    sent.extend(start(AG_B, lambda q: s_agb, r_agb))
    r_agb[me] = s_agb[...]
    grad_ref[...] = total.T
    store(2)
    for row in range(nblk * nsub):
        source = row * nch + my_row // share

        @pl.when(source != me)
        def _():
            pltpu.make_async_remote_copy(
                src_ref=r_col.at[row],
                dst_ref=r_col.at[row],
                send_sem=col_send.at[0],
                recv_sem=col_recv.at[row],
                device_id=place(row, my_row // share),
                device_id_type=pl.DeviceIdType.MESH,
            ).wait_recv()

        for j in range(half_rows):
            x = wide(r_col[row])[j * rows : (j + 1) * rows]
            swap_f32[j, row * rows : (row + 1) * rows, :] = x[:, 0:lanes]
            swap_f32[j + half_rows, row * rows : (row + 1) * rows, :] = x[:, lanes:width]
    for j in range(rows):
        swapped_ref[j] = low(swap_f32[j].T)
    store(1)
    arrive(AG_B, None, r_agb)
    for q in range(n):
        x = wide(r_agb[q])
        at = q * per
        g_proj_ref[at : at + per, :] = x[0:per, 0 : 2 * width]
        g_gate_ref[at : at + per, :] = x[per : 2 * per, 0 : 2 * width]
        g_gout_ref[at : at + per, :] = x[0:per, 2 * width : 3 * width]
        g_out_ref[at : at + per, :] = x[per : 2 * per, 2 * width : 3 * width]

    for q in range(3, 7):
        store(q)
    for copy in sent:
        copy.wait_send()
    for m in range(share):
        for col in range(nch):
            slot = m * nch + col
            row = my_ch * share + m

            @pl.when(row * nch + col != me)
            def _():
                col_copy(slot, row, col).wait_send()

    for q in range(7):
        pltpu.make_async_copy(made[q], outputs[q], store_sem.at[q]).wait()


def write_kernel(count, *refs):
    source, target, held = refs[:count], refs[count : 2 * count], refs[2 * count : 3 * count]
    come, go = refs[3 * count :]
    arriving = [pltpu.make_async_copy(source[q], held[q], come.at[q]) for q in range(count)]
    leaving = [pltpu.make_async_copy(held[q], target[q], go.at[q]) for q in range(count)]
    for copy in arriving:
        copy.start()
    for one, other in zip(arriving, leaving):
        one.wait()
        other.start()
    for copy in leaving:
        copy.wait()


def write_out(values):
    count = len(values)
    return pl.pallas_call(
        functools.partial(write_kernel, count),
        out_shape=tuple(jax.ShapeDtypeStruct(x.shape, x.dtype) for x in values),
        in_specs=[pl.BlockSpec(memory_space=pltpu.HBM)] * count,
        out_specs=[pl.BlockSpec(memory_space=pltpu.HBM)] * count,
        scratch_shapes=[pltpu.VMEM(x.shape, x.dtype) for x in values]
        + [pltpu.SemaphoreType.DMA((count,))] * 2,
        compiler_params=pltpu.CompilerParams(vmem_limit_bytes=most_vmem),
    )(*values)


def fused(
    sizes,
    pair_in,
    cotangent,
    chain_ids,
    live_length,
    chain_embed,
    gain_in,
    bias_in,
    w_proj,
    w_gate,
    w_gout,
    gain_out,
    bias_out,
    w_out,
):
    rows, cols, width = pair_in.shape
    n = sizes["blk"] * sizes["sub"] * sizes["ch"]
    per = width // n
    cells, tokens, lanes = rows * cols, cols * sizes["ch"], width // sizes["ch"]
    half = cells // 2
    slots = cols // rows * sizes["ch"]
    col_rows = -(-(rows // 2 * rows) // 16) * 16
    bf, f32 = jnp.bfloat16, jnp.float32
    vm = pltpu.VMEM

    def both(*shape):
        return [vm((n,) + shape, bf), vm((n,) + shape, bf)]

    line = lambda x: x.reshape(1, -1)
    operands = (
        pair_in.reshape(cells, width),
        cotangent.reshape(cells, width),
        line(chain_ids),
        line(chain_embed),
        line(gain_in),
        line(bias_in),
        line(gain_out),
        line(bias_out),
        w_proj,
        w_gate,
        w_gout,
        w_out,
    )
    results = (
        jax.ShapeDtypeStruct((cells, width), bf),
        jax.ShapeDtypeStruct((rows, lanes, tokens), bf),
        jax.ShapeDtypeStruct((cells, width), f32),
        jax.ShapeDtypeStruct((width, 2 * width), f32),
        jax.ShapeDtypeStruct((width, 2 * width), f32),
        jax.ShapeDtypeStruct((width, width), f32),
        jax.ShapeDtypeStruct((width, width), f32),
    )
    outs = pl.pallas_call(
        functools.partial(kernel, sizes, rows, cols),
        out_shape=results,
        in_specs=[pl.BlockSpec(memory_space=pltpu.SMEM)]
        + [pl.BlockSpec(memory_space=pltpu.HBM)] * 12,
        out_specs=[pl.BlockSpec(memory_space=pltpu.HBM)] * 7,
        scratch_shapes=[vm(x.shape, x.dtype) for x in operands + results]
        + both(2 * per, cells)
        + both(2 * per, half)
        + both(2 * per, half)
        + both(2 * per, cells)
        + both(2 * per, width)
        + both(2 * per, 2 * width)
        + [vm((2 * per, 3 * width), bf), vm((n, 2 * per, 3 * width), bf)]
        + [vm((slots, col_rows, width), bf), vm((n // sizes["ch"], col_rows, width), bf)]
        + [
            vm((width, cells), f32),
            vm((width, cells), bf),
            vm((2 * width, cells), f32),
            vm((2 * width, cells), f32),
            vm((width, cells), f32),
            vm((width, cells), bf),
            vm((width, cells), f32),
            vm((width, cells), bf),
            vm((tokens * 2 * per, tokens), f32),
            vm((tokens * per, tokens), f32),
            vm((per, tokens, tokens), bf),
            vm((per, tokens, tokens), bf),
            vm((n, 2 * per, cells), f32),
            vm((n, 2 * per, half), f32),
            vm((width, cells), f32),
            vm((cells, width), f32),
            vm((slots, col_rows, width), f32),
            vm((rows, tokens, lanes), f32),
            pltpu.SemaphoreType.DMA((PHASES, n)),
            pltpu.SemaphoreType.DMA((PHASES, n)),
            pltpu.SemaphoreType.DMA((slots,)),
            pltpu.SemaphoreType.DMA((n // sizes["ch"],)),
            pltpu.SemaphoreType.DMA((12,)),
            pltpu.SemaphoreType.DMA((7,)),
        ],
        compiler_params=pltpu.CompilerParams(
            collective_id=0, has_side_effects=True, vmem_limit_bytes=most_vmem
        ),
    )(line(live_length), *operands)
    outs = write_out(outs)
    new_pair, pair_cols, grad_pair, *grads = outs
    return (
        new_pair.reshape(rows, cols, width),
        jnp.swapaxes(pair_cols, 1, 2),
        grad_pair.reshape(rows, cols, width),
        *grads,
    )


def solution(mesh):
    sizes = dict(mesh.shape)
    devices = sizes["blk"] * sizes["sub"] * sizes["ch"]
    fits = devices * 8 == 128 and sizes["ch"] == 2
    body = functools.partial(fused, sizes) if fits else on_device
    return jax.shard_map(
        body,
        mesh=mesh,
        in_specs=(
            P(("grp", "blk", "sub"), "ch", None),
            P(("grp", "blk", "sub"), "ch", None),
            P("grp"),
            P("grp"),
            P(),
            P(),
            P(),
            P(),
            P(),
            P(),
            P(),
            P(),
            P(),
        ),
        out_specs=(
            P(("grp", "blk", "sub"), "ch", None),
            P(("grp", "blk", "sub"), None, "ch"),
            P(("grp", "blk", "sub"), "ch", None),
            P("grp", None),
            P("grp", None),
            P("grp", None),
            P("grp", None),
        ),
        check_vma=False,
    )
```

```python
import functools

import jax
import jax.numpy as jnp
from jax import lax
from jax.experimental import pallas as pl
from jax.experimental.pallas import tpu as pltpu
from jax.sharding import PartitionSpec as P

eps = 1e-05


def norm_affine(field, gain, bias):
    mean = jnp.mean(field, axis=-1, keepdims=True)
    centred = field - mean
    spread = jnp.mean(centred * centred, axis=-1, keepdims=True)
    return centred * lax.rsqrt(spread + eps) * gain + bias


def flat_grad(left_cells, right_cells, width_left, width_right):
    left_flat = left_cells.reshape(-1, width_left)
    right_flat = right_cells.reshape(-1, width_right)
    right_high = right_flat.astype(jnp.bfloat16)
    right_low = (right_flat - right_high.astype(jnp.float32)).astype(jnp.bfloat16)
    dims = (((0,), (0,)), ((), ()))
    upper = lax.dot_general(left_flat, right_high, dims, preferred_element_type=jnp.float32)
    lower = lax.dot_general(left_flat, right_low, dims, preferred_element_type=jnp.float32)
    return upper + lower


def fold_right(right_ch, update, initial):
    return update(
        initial, lax.all_gather(right_ch, ("blk", "sub"), axis=0, tiled=True), jnp.int32(0)
    )


def on_device(
    pair_in,
    cotangent,
    chain_ids,
    live_length,
    chain_embed,
    gain_in,
    bias_in,
    w_proj,
    w_gate,
    w_gout,
    gain_out,
    bias_out,
    w_out,
):
    row_count = pair_in.shape[0]
    col_count = pair_in.shape[1]
    width = pair_in.shape[2]
    row_start = lax.axis_index(("blk", "sub")) * row_count
    col_start = lax.axis_index("ch") * col_count
    row_pos = row_start + jnp.arange(row_count, dtype=jnp.int32)
    col_pos = col_start + jnp.arange(col_count, dtype=jnp.int32)
    live_rows = (row_pos < live_length[0]).astype(jnp.float32)
    live_cols = (col_pos < live_length[0]).astype(jnp.float32)
    cell_mask = (live_rows[:, None] * live_cols[None, :])[..., None]
    chain_rows = lax.dynamic_slice_in_dim(chain_ids, row_start, row_count)
    chain_cols = lax.dynamic_slice_in_dim(chain_ids, col_start, col_count)
    same = (chain_rows[:, None] == chain_cols[None, :]).astype(jnp.float32)
    pair = pair_in.astype(jnp.float32) + same[..., None] * chain_embed
    normed, back_in = jax.vjp(lambda field: norm_affine(field, gain_in, bias_in), pair)
    normed_cast = normed.astype(jnp.bfloat16)
    projected = jnp.dot(normed_cast, w_proj, preferred_element_type=jnp.float32)
    gate_pre = jnp.dot(normed_cast, w_gate, preferred_element_type=jnp.float32)
    gout_pre = jnp.dot(normed_cast, w_gout, preferred_element_type=jnp.float32)
    gate_sig = jax.nn.sigmoid(gate_pre)
    gout = jax.nn.sigmoid(gout_pre)
    operands = (projected * gate_sig * cell_mask).astype(jnp.bfloat16)
    left_ch, right_ch = (
        lax.all_to_all(operands[..., :width], "ch", split_axis=2, concat_axis=1, tiled=True),
        lax.all_to_all(operands[..., width:], "ch", split_axis=2, concat_axis=1, tiled=True),
    )

    def add_tri(carry, piece, start):
        update = jnp.einsum("ikc,jkc->ijc", left_ch, piece, preferred_element_type=jnp.float32)
        return update

    tri_sum = fold_right(right_ch, add_tri, jnp.zeros(left_ch.shape, jnp.float32))
    tri_cast = tri_sum.astype(jnp.bfloat16)
    tri_cells = lax.all_to_all(tri_cast, "ch", split_axis=1, concat_axis=2, tiled=True)
    outnorm, back_out = jax.vjp(
        lambda field: norm_affine(field, gain_out, bias_out), tri_cells.astype(jnp.float32)
    )
    outnorm_cast = outnorm.astype(jnp.bfloat16)
    out_lin = jnp.dot(outnorm_cast, w_out, preferred_element_type=jnp.float32)
    new_pair = (pair + out_lin * gout).astype(jnp.bfloat16)
    swapped = lax.all_to_all(
        lax.all_to_all(new_pair, "ch", split_axis=2, concat_axis=1, tiled=True),
        ("blk", "sub"),
        split_axis=1,
        concat_axis=0,
        tiled=True,
    )
    pair_cols = jnp.transpose(swapped, (1, 0, 2))
    d_new = cotangent.astype(jnp.float32)
    d_lin = d_new * gout
    d_gout_pre = d_new * out_lin * gout * (1.0 - gout)
    local_w_out = flat_grad(outnorm_cast, d_lin, width, width)
    d_norm = jnp.dot(d_lin, w_out.astype(jnp.float32).T, precision=lax.Precision.HIGHEST)
    (d_tri,) = back_out(d_norm)
    d_tri_cast = d_tri.astype(jnp.bfloat16)
    d_tri_ch = lax.all_to_all(d_tri_cast, "ch", split_axis=2, concat_axis=1, tiled=True)

    def add_left(carry, piece, start):
        return jnp.einsum("ijc,jkc->ikc", d_tri_ch, piece, preferred_element_type=jnp.float32)

    d_left = fold_right(right_ch, add_left, jnp.zeros(left_ch.shape, jnp.float32))
    d_tri_swap = lax.all_to_all(d_tri_ch, ("blk", "sub"), split_axis=1, concat_axis=0, tiled=True)
    d_right = jnp.einsum(
        "ijc,ikc->jkc",
        d_tri_swap,
        lax.all_gather(left_ch, ("blk", "sub"), axis=0, tiled=True),
        preferred_element_type=jnp.float32,
    )
    back_left, back_right = (
        lax.all_to_all(d_left.astype(jnp.bfloat16), "ch", split_axis=1, concat_axis=2, tiled=True),
        lax.all_to_all(d_right.astype(jnp.bfloat16), "ch", split_axis=1, concat_axis=2, tiled=True),
    )
    d_operands = jnp.concatenate([back_left, back_right], axis=-1).astype(jnp.float32)
    d_proj = d_operands * gate_sig * cell_mask
    d_gate = d_operands * projected * gate_sig * (1.0 - gate_sig) * cell_mask
    local_w_proj = flat_grad(normed_cast, d_proj, width, 2 * width)
    local_w_gate = flat_grad(normed_cast, d_gate, width, 2 * width)
    local_w_gout = flat_grad(normed_cast, d_gout_pre, width, width)
    highest = lax.Precision.HIGHEST
    d_normed = jnp.dot(d_proj, w_proj.astype(jnp.float32).T, precision=highest)
    d_normed = d_normed + jnp.dot(d_gate, w_gate.astype(jnp.float32).T, precision=highest)
    d_normed = d_normed + jnp.dot(d_gout_pre, w_gout.astype(jnp.float32).T, precision=highest)
    (d_pair,) = back_in(d_normed)
    grad_pair = d_new + d_pair
    grad_w_proj, grad_w_gate, grad_w_gout, grad_w_out = lax.psum(
        (local_w_proj, local_w_gate, local_w_gout, local_w_out), ("blk", "ch", "sub")
    )
    return (new_pair, pair_cols, grad_pair, grad_w_proj, grad_w_gate, grad_w_gout, grad_w_out)


most_vmem = (64 << 20) - (96 << 10)

OPS, TRI, DTRI, DOPS, RS_A, RS_B, AG_B, PHASES = range(8)


def column_norm(field):
    mean = jnp.mean(field, axis=0, keepdims=True)
    centred = field - mean
    spread = jnp.mean(centred * centred, axis=0, keepdims=True)
    scale = lax.rsqrt(spread + eps)
    return centred * scale, scale


def column_norm_back(unit, scale, d_unit):
    first = jnp.mean(d_unit, axis=0, keepdims=True)
    second = jnp.mean(d_unit * unit, axis=0, keepdims=True)
    return scale * (d_unit - first - unit * second)


def matmul(a, b, dims=((1,), (0,))):
    return lax.dot_general(a, b, (dims, ((), ())), preferred_element_type=jnp.float32)


def low(x):
    return x.astype(jnp.bfloat16)


def wide(x):
    return x.astype(jnp.float32)


def kernel(
    sizes,
    rows,
    cols,
    live_ref,
    *refs,
):
    inputs, outputs, scratch = refs[:12], refs[12:19], refs[19:]
    loaded, made, scratch = scratch[:12], scratch[12:19], scratch[19:]
    (
    pair_ref,
    cot_ref,
    chain_ref,
    embed_ref,
    gain_in_ref,
    bias_in_ref,
    gain_out_ref,
    bias_out_ref,
    w_proj_ref,
    w_gate_ref,
    w_gout_ref,
    w_out_ref,
    ) = loaded
    (
    new_ref,
    swapped_ref,
    grad_ref,
    g_proj_ref,
    g_gate_ref,
    g_gout_ref,
    g_out_ref,
    ) = made
    (
    s_ops, r_ops, s_tri, r_tri, s_dtri, r_dtri, s_dops, r_dops,
    s_rsa, r_rsa, s_rsb, r_rsb, s_agb, r_agb,
    s_col, r_col,
    pair_buf, normed_buf, proj_buf, gate_buf, gout_buf, dlin_buf, dnew_buf, dgout_buf,
    pairs16, pairs8, left_buf, right_buf, flat16, flat8, cells_buf, rows_buf, col_f32, swap_f32,
    send_sem, recv_sem, col_send, col_recv, load_sem, store_sem,
    ) = scratch
    nblk, nsub, nch = sizes["blk"], sizes["sub"], sizes["ch"]
    n = nblk * nsub * nch
    width = pair_ref.shape[1]
    per = width // n
    cells = rows * cols
    half = cells // 2
    half_rows = rows // 2
    tokens = cols * nch
    my_row = lax.axis_index("blk") * nsub + lax.axis_index("sub")
    my_ch = lax.axis_index("ch")
    me = my_row * nch + my_ch

    def place(row, col):
        return {"blk": row // nsub, "sub": row % nsub, "ch": col}

    def partner(t):
        q, bit = me, 1
        while bit <= t:
            if t & bit:
                q = q + bit * (1 - 2 * (me // bit % 2))
            bit *= 2
        return q

    def start(phase, src_of, dst):
        copies = []
        for t in reversed(range(1, n)):
            q = partner(t)
            copy = pltpu.make_async_remote_copy(
                src_ref=src_of(q),
                dst_ref=dst.at[me],
                send_sem=send_sem.at[phase, t],
                recv_sem=recv_sem.at[phase, t],
                device_id=place(q // nch, q % nch),
                device_id_type=pl.DeviceIdType.MESH,
            )
            copy.start()
            copies.append(copy)
        return copies

    def arrive(phase, copies, dst):
        for t in range(1, n):
            q = partner(t)
            pltpu.make_async_remote_copy(
                src_ref=dst.at[q],
                dst_ref=dst.at[q],
                send_sem=send_sem.at[phase, t],
                recv_sem=recv_sem.at[phase, t],
                device_id=place(q // nch, q % nch),
                device_id_type=pl.DeviceIdType.MESH,
            ).wait_recv()

    sent = []

    def store(q):
        pltpu.make_async_copy(made[q], outputs[q], store_sem.at[q]).start()

    def exchange(phase, src, dst):
        sent.extend(start(phase, lambda q: src.at[q], dst))
        dst[me] = src[me]

    barrier = pltpu.get_barrier_semaphore()
    for t in range(1, n):
        q = partner(t)
        pl.semaphore_signal(
            barrier,
            inc=1,
            device_id=place(q // nch, q % nch),
            device_id_type=pl.DeviceIdType.MESH,
        )

    loads = [
        pltpu.make_async_copy(inputs[q], loaded[q], load_sem.at[q]) for q in range(12)
    ]
    for load in loads:
        load.start()
    for load in loads:
        load.wait()

    vectors = jnp.concatenate(
        [
            embed_ref[...],
            gain_in_ref[...],
            bias_in_ref[...],
            gain_out_ref[...],
            bias_out_ref[...],
            jnp.zeros((3, width), jnp.float32),
        ],
        axis=0,
    ).T
    embed, gain_in, bias_in, gain_out, bias_out = [vectors[:, q : q + 1] for q in range(5)]

    cell = lax.broadcasted_iota(jnp.int32, (tokens, cells), 1)
    token = lax.broadcasted_iota(jnp.int32, (tokens, cells), 0)
    local_row = jnp.zeros((tokens, cells), jnp.int32)
    for q in range(1, rows):
        local_row = local_row + (cell >= q * cols).astype(jnp.int32)
    row_pos = my_row * rows + local_row
    col_pos = my_ch * cols + cell - local_row * cols
    pick = (token == row_pos).astype(jnp.float32) - (token == col_pos).astype(jnp.float32)
    chain = jnp.broadcast_to(wide(chain_ref[...]), (8, tokens))
    apart = matmul(low(chain), low(pick))[0:1]
    same = (apart == 0.0).astype(jnp.float32)
    length = live_ref[0, 0]
    mask = (row_pos[0:1] < length).astype(jnp.float32) * (col_pos[0:1] < length).astype(jnp.float32)

    pair = wide(pair_ref[...]).T + same * embed
    pair_buf[...] = pair
    unit_in, scale_in = column_norm(pair)
    normed = low(unit_in * gain_in + bias_in)
    normed_buf[...] = normed
    projected = matmul(low(wide(w_proj_ref[...]).T), normed)
    gate_sig = jax.nn.sigmoid(matmul(low(wide(w_gate_ref[...]).T), normed))
    masked = gate_sig * mask
    operands = projected * masked
    gate_buf[...] = masked
    proj_buf[...] = operands * (1.0 - gate_sig)
    for q in range(n):
        low_q, high_q = q * per, width + q * per
        s_ops[q] = low(
            jnp.concatenate(
                [operands[low_q : low_q + per], operands[high_q : high_q + per]], axis=0
            )
        )
    pl.semaphore_wait(barrier, n - 1)
    exchange(OPS, s_ops, r_ops)

    gout = jax.nn.sigmoid(matmul(low(wide(w_gout_ref[...]).T), normed))
    gout_buf[...] = gout
    d_new = wide(cot_ref[...]).T
    dnew_buf[...] = d_new
    d_lin = low(d_new * gout)
    dlin_buf[...] = d_lin
    d_unit_out = matmul(w_out_ref[...], d_lin) * gain_out
    w_out_t = low(wide(w_out_ref[...]).T)

    arrive(OPS, None, r_ops)
    for q in range(n):
        block_row, block_col = q // nch, q % nch
        x = wide(r_ops[q])
        for i in range(rows):
            at = (block_row * rows + i) * 2 * per
            pairs16[at : at + 2 * per, block_col * cols : (block_col + 1) * cols] = x[
                :, i * cols : (i + 1) * cols
            ]
    for c in range(per):
        left = low(pairs16[pl.ds(c, tokens, stride=2 * per), :])
        right = low(pairs16[pl.ds(per + c, tokens, stride=2 * per), :])
        left_buf[c] = left
        right_buf[c] = right
        pairs8[pl.ds(c, tokens, stride=per), :] = matmul(left, right, ((1,), (1,)))
    for q in range(n):
        block_row, block_col = q // nch, q % nch
        for i in range(rows):
            at = (block_row * rows + i) * per
            down, along = (i // half_rows) * per, (i % half_rows) * cols
            flat8[q, down : down + per, along : along + cols] = pairs8[
                at : at + per, block_col * cols : (block_col + 1) * cols
            ]
        s_tri[q] = low(flat8[q])
    exchange(TRI, s_tri, r_tri)
    arrive(TRI, None, r_tri)
    for q in range(n):
        x = wide(r_tri[q])
        cells_buf[q * per : (q + 1) * per, 0:half] = x[0:per]
        cells_buf[q * per : (q + 1) * per, half:cells] = x[per : 2 * per]

    unit_out, scale_out = column_norm(cells_buf[...])
    d_tri = column_norm_back(unit_out, scale_out, d_unit_out)
    for q in range(n):
        x = d_tri[q * per : (q + 1) * per]
        s_dtri[q] = low(jnp.concatenate([x[:, 0:half], x[:, half:cells]], axis=0))
    exchange(DTRI, s_dtri, r_dtri)

    outnorm = low(unit_out * gain_out + bias_out)
    out_lin = matmul(w_out_t, outnorm)
    gout = gout_buf[...]
    moved = out_lin * gout
    d_gout = low(dnew_buf[...] * moved * (1.0 - gout))
    dgout_buf[...] = d_gout
    grad_gout = matmul(normed_buf[...], d_gout, ((1,), (1,)))
    grad_out = matmul(outnorm, dlin_buf[...], ((1,), (1,)))
    for q in range(n):
        at = q * per
        s_rsa[q] = low(
            jnp.concatenate([grad_gout[at : at + per], grad_out[at : at + per]], axis=0)
        )
    exchange(RS_A, s_rsa, r_rsa)

    new_rows = (pair_buf[...] + moved).T
    rows_buf[0:cells, :] = new_rows
    new_ref[...] = low(new_rows)
    store(0)
    share = cols // rows
    lanes = width // nch
    first = lax.broadcasted_iota(jnp.int32, (rows, width), 1) < lanes
    for m in range(share):
        for j in range(half_rows):
            a = rows_buf[pl.ds(m * rows + j, rows, stride=cols), :]
            b = rows_buf[pl.ds(m * rows + j + half_rows, rows, stride=cols), :]
            col_f32[m * nch, j * rows : (j + 1) * rows, :] = jnp.where(
                first, a, pltpu.roll(b, lanes, 1)
            )
            col_f32[m * nch + 1, j * rows : (j + 1) * rows, :] = jnp.where(
                first, pltpu.roll(a, lanes, 1), b
            )
        for col in range(nch):
            used = half_rows * rows
            spare = col_f32.shape[1] - used
            if spare:
                col_f32[m * nch + col, used : used + spare, :] = jnp.zeros(
                    (spare, width), jnp.float32
                )
            s_col[m * nch + col] = low(col_f32[m * nch + col])

    def col_copy(slot, row, col):
        return pltpu.make_async_remote_copy(
            src_ref=s_col.at[slot],
            dst_ref=r_col.at[my_row],
            send_sem=col_send.at[slot],
            recv_sem=col_recv.at[my_row],
            device_id=place(row, col),
            device_id_type=pl.DeviceIdType.MESH,
        )

    for m in range(share // 2):
        for col in range(nch):
            slot = m * nch + col
            row = my_ch * share + m
            here = row * nch + col == me

            @pl.when(here)
            def _():
                r_col[my_row] = s_col[slot]

            @pl.when(jnp.logical_not(here))
            def _():
                col_copy(slot, row, col).start()

    arrive(DTRI, None, r_dtri)
    for q in range(n):
        block_row, block_col = q // nch, q % nch
        x = wide(r_dtri[q])
        for i in range(rows):
            at = (block_row * rows + i) * per
            down, along = (i // half_rows) * per, (i % half_rows) * cols
            pairs8[at : at + per, block_col * cols : (block_col + 1) * cols] = x[
                down : down + per, along : along + cols
            ]
    for c in range(per):
        grad = pairs8[pl.ds(c, tokens, stride=per), :]
        pairs16[pl.ds(c, tokens, stride=2 * per), :] = matmul(low(grad), right_buf[c])
        pairs16[pl.ds(per + c, tokens, stride=2 * per), :] = matmul(low(grad.T), left_buf[c])
    for q in range(n):
        block_row, block_col = q // nch, q % nch
        for i in range(rows):
            at = (block_row * rows + i) * 2 * per
            flat16[q, :, i * cols : (i + 1) * cols] = pairs16[
                at : at + 2 * per, block_col * cols : (block_col + 1) * cols
            ]
        s_dops[q] = low(flat16[q])
    exchange(DOPS, s_dops, r_dops)
    for m in range(share // 2, share):
        for col in range(nch):
            slot = m * nch + col
            row = my_ch * share + m
            here = row * nch + col == me

            @pl.when(here)
            def _():
                r_col[my_row] = s_col[slot]

            @pl.when(jnp.logical_not(here))
            def _():
                col_copy(slot, row, col).start()

    def summed(buf):
        total = wide(buf[0])
        for q in range(1, n):
            total = total + wide(buf[q])
        return low(total)

    d_normed_gout = matmul(w_gout_ref[...], dgout_buf[...])

    arrive(DOPS, None, r_dops)
    d_operands = jnp.concatenate(
        [wide(r_dops[q])[0:per] for q in range(n)]
        + [wide(r_dops[q])[per : 2 * per] for q in range(n)],
        axis=0,
    )
    d_proj = low(d_operands * gate_buf[...])
    d_gate = low(d_operands * proj_buf[...])
    normed = normed_buf[...]
    grad_proj = matmul(normed, d_proj, ((1,), (1,)))
    grad_gate = matmul(normed, d_gate, ((1,), (1,)))
    for q in range(n):
        at = q * per
        s_rsb[q] = low(
            jnp.concatenate([grad_proj[at : at + per], grad_gate[at : at + per]], axis=0)
        )
    exchange(RS_B, s_rsb, r_rsb)

    d_normed = d_normed_gout + matmul(w_proj_ref[...], d_proj) + matmul(w_gate_ref[...], d_gate)
    unit_in, scale_in = column_norm(pair_buf[...])
    d_pair = column_norm_back(unit_in, scale_in, d_normed * gain_in)
    total = dnew_buf[...] + d_pair

    arrive(RS_B, None, r_rsb)
    arrive(RS_A, None, r_rsa)
    s_agb[:, 0 : 2 * width] = summed(r_rsb)
    s_agb[:, 2 * width : 3 * width] = summed(r_rsa)
    sent.extend(start(AG_B, lambda q: s_agb, r_agb))
    r_agb[me] = s_agb[...]
    grad_ref[...] = total.T
    store(2)
    for row in range(nblk * nsub):
        source = row * nch + my_row // share

        @pl.when(source != me)
        def _():
            pltpu.make_async_remote_copy(
                src_ref=r_col.at[row],
                dst_ref=r_col.at[row],
                send_sem=col_send.at[0],
                recv_sem=col_recv.at[row],
                device_id=place(row, my_row // share),
                device_id_type=pl.DeviceIdType.MESH,
            ).wait_recv()

        for j in range(half_rows):
            x = wide(r_col[row])[j * rows : (j + 1) * rows]
            swap_f32[j, row * rows : (row + 1) * rows, :] = x[:, 0:lanes]
            swap_f32[j + half_rows, row * rows : (row + 1) * rows, :] = x[:, lanes:width]
    for j in range(rows):
        swapped_ref[j] = low(swap_f32[j].T)
    store(1)
    arrive(AG_B, None, r_agb)
    for q in range(n):
        x = wide(r_agb[q])
        at = q * per
        g_proj_ref[at : at + per, :] = x[0:per, 0 : 2 * width]
        g_gate_ref[at : at + per, :] = x[per : 2 * per, 0 : 2 * width]
        g_gout_ref[at : at + per, :] = x[0:per, 2 * width : 3 * width]
        g_out_ref[at : at + per, :] = x[per : 2 * per, 2 * width : 3 * width]

    for q in range(3, 7):
        store(q)
    for copy in sent:
        copy.wait_send()
    for m in range(share):
        for col in range(nch):
            slot = m * nch + col
            row = my_ch * share + m

            @pl.when(row * nch + col != me)
            def _():
                col_copy(slot, row, col).wait_send()

    for q in range(7):
        pltpu.make_async_copy(made[q], outputs[q], store_sem.at[q]).wait()


def write_kernel(count, *refs):
    source, target, held = refs[:count], refs[count : 2 * count], refs[2 * count : 3 * count]
    come, go = refs[3 * count :]
    arriving = [pltpu.make_async_copy(source[q], held[q], come.at[q]) for q in range(count)]
    leaving = [pltpu.make_async_copy(held[q], target[q], go.at[q]) for q in range(count)]
    for copy in arriving:
        copy.start()
    for one, other in zip(arriving, leaving):
        one.wait()
        other.start()
    for copy in leaving:
        copy.wait()


def write_out(values):
    count = len(values)
    return pl.pallas_call(
        functools.partial(write_kernel, count),
        out_shape=tuple(jax.ShapeDtypeStruct(x.shape, x.dtype) for x in values),
        in_specs=[pl.BlockSpec(memory_space=pltpu.HBM)] * count,
        out_specs=[pl.BlockSpec(memory_space=pltpu.HBM)] * count,
        scratch_shapes=[pltpu.VMEM(x.shape, x.dtype) for x in values]
        + [pltpu.SemaphoreType.DMA((count,))] * 2,
        compiler_params=pltpu.CompilerParams(vmem_limit_bytes=most_vmem),
    )(*values)


def fused(
    sizes,
    pair_in,
    cotangent,
    chain_ids,
    live_length,
    chain_embed,
    gain_in,
    bias_in,
    w_proj,
    w_gate,
    w_gout,
    gain_out,
    bias_out,
    w_out,
):
    rows, cols, width = pair_in.shape
    n = sizes["blk"] * sizes["sub"] * sizes["ch"]
    per = width // n
    cells, tokens, lanes = rows * cols, cols * sizes["ch"], width // sizes["ch"]
    half = cells // 2
    slots = cols // rows * sizes["ch"]
    col_rows = -(-(rows // 2 * rows) // 16) * 16
    bf, f32 = jnp.bfloat16, jnp.float32
    vm = pltpu.VMEM

    def both(*shape):
        return [vm((n,) + shape, bf), vm((n,) + shape, bf)]

    line = lambda x: x.reshape(1, -1)
    operands = (
        pair_in.reshape(cells, width),
        cotangent.reshape(cells, width),
        line(chain_ids),
        line(chain_embed),
        line(gain_in),
        line(bias_in),
        line(gain_out),
        line(bias_out),
        w_proj,
        w_gate,
        w_gout,
        w_out,
    )
    results = (
        jax.ShapeDtypeStruct((cells, width), bf),
        jax.ShapeDtypeStruct((rows, lanes, tokens), bf),
        jax.ShapeDtypeStruct((cells, width), f32),
        jax.ShapeDtypeStruct((width, 2 * width), f32),
        jax.ShapeDtypeStruct((width, 2 * width), f32),
        jax.ShapeDtypeStruct((width, width), f32),
        jax.ShapeDtypeStruct((width, width), f32),
    )
    outs = pl.pallas_call(
        functools.partial(kernel, sizes, rows, cols),
        out_shape=results,
        in_specs=[pl.BlockSpec(memory_space=pltpu.SMEM)]
        + [pl.BlockSpec(memory_space=pltpu.HBM)] * 12,
        out_specs=[pl.BlockSpec(memory_space=pltpu.HBM)] * 7,
        scratch_shapes=[vm(x.shape, x.dtype) for x in operands + results]
        + both(2 * per, cells)
        + both(2 * per, half)
        + both(2 * per, half)
        + both(2 * per, cells)
        + both(2 * per, width)
        + both(2 * per, 2 * width)
        + [vm((2 * per, 3 * width), bf), vm((n, 2 * per, 3 * width), bf)]
        + [vm((slots, col_rows, width), bf), vm((n // sizes["ch"], col_rows, width), bf)]
        + [
            vm((width, cells), f32),
            vm((width, cells), bf),
            vm((2 * width, cells), f32),
            vm((2 * width, cells), f32),
            vm((width, cells), f32),
            vm((width, cells), bf),
            vm((width, cells), f32),
            vm((width, cells), bf),
            vm((tokens * 2 * per, tokens), f32),
            vm((tokens * per, tokens), f32),
            vm((per, tokens, tokens), bf),
            vm((per, tokens, tokens), bf),
            vm((n, 2 * per, cells), f32),
            vm((n, 2 * per, half), f32),
            vm((width, cells), f32),
            vm((-(-rows // 8) * 8 * cols, width), f32),
            vm((slots, col_rows, width), f32),
            vm((rows, tokens, lanes), f32),
            pltpu.SemaphoreType.DMA((PHASES, n)),
            pltpu.SemaphoreType.DMA((PHASES, n)),
            pltpu.SemaphoreType.DMA((slots,)),
            pltpu.SemaphoreType.DMA((n // sizes["ch"],)),
            pltpu.SemaphoreType.DMA((12,)),
            pltpu.SemaphoreType.DMA((7,)),
        ],
        compiler_params=pltpu.CompilerParams(
            collective_id=0, has_side_effects=True, vmem_limit_bytes=most_vmem
        ),
    )(line(live_length), *operands)
    outs = write_out(outs)
    new_pair, pair_cols, grad_pair, *grads = outs
    return (
        new_pair.reshape(rows, cols, width),
        jnp.swapaxes(pair_cols, 1, 2),
        grad_pair.reshape(rows, cols, width),
        *grads,
    )


def solution(mesh):
    sizes = dict(mesh.shape)
    devices = sizes["blk"] * sizes["sub"] * sizes["ch"]
    fits = devices * 8 == 128 and sizes["ch"] == 2
    body = functools.partial(fused, sizes) if fits else on_device
    return jax.shard_map(
        body,
        mesh=mesh,
        in_specs=(
            P(("grp", "blk", "sub"), "ch", None),
            P(("grp", "blk", "sub"), "ch", None),
            P("grp"),
            P("grp"),
            P(),
            P(),
            P(),
            P(),
            P(),
            P(),
            P(),
            P(),
            P(),
        ),
        out_specs=(
            P(("grp", "blk", "sub"), "ch", None),
            P(("grp", "blk", "sub"), None, "ch"),
            P(("grp", "blk", "sub"), "ch", None),
            P("grp", None),
            P("grp", None),
            P("grp", None),
            P("grp", None),
        ),
        check_vma=False,
    )
```
